32 devices in a mesh: parts: 2 (over x), slab: 16 (over z, y, core).
Axes of the slice: x: 2, y: 2, z: 4, core: 2. Of those that a mesh axis runs over, the one named last changes fastest.
Arguments:
- volume: float32 [64, 2048, 128], P(('parts', 'slab')), parts along dimension 0, may hold values from -6 to 6
- voxel_weight: float32 [64, 2048, 128], P(('parts', 'slab')), parts along dimension 0, may hold values from 0.02 to 0.2
- measured: float32 [16, 256, 128], P('parts', 'slab'), parts along dimension 0, may hold values from -96 to 96
- ray_weight: float32 [256, 128], replicated, may hold values from 0.02 to 0.2
- footprint: bfloat16 [8, 2, 128, 128], replicated, may hold values from -0.5 to 0.5
- hits: int32 [64, 2048, 8, 2], P(('parts', 'slab')), parts along dimension 0, may hold values from 0 to 255, as said below
Outputs:
- smoothed: float32 [64, 2048, 128], P(('parts', 'slab')), parts along dimension 0
The draws below stay inside these ranges and needn't reach their ends.
There are 2 independent parts, one for each index of `parts`. The reference program is written for one: setup_inputs(seed, part) draws one part's arguments, and reference() takes and returns one part's arrays. A program takes and returns all parts, laid end to end along the dimension named above; an argument that names none is the same for every part. Nothing has to cross between parts.
Inputs may be any that keep to these rules, and one draw needn't show every extreme that they name: hits[z, t, a, k] = hits[z, t, a, 0] + k.
All inputs are finite; a program needn't handle non-finite values.
Results may differ from the reference program's by a relative error of at most 0.0042.
Values may be sent and summed in bfloat16 or wider, within the bound.
No kernel may reach another device: no remote copies, remote signals or barrier semaphores. Data moves between devices by JAX's collectives and lax.ppermute only.
A program may use at most 64 MiB of HBM per device.

```python
import math
import jax
import jax.numpy as jnp
from jax import lax

TILE = 128
BIN = 128
XT = 2048
SUBSET = 4
ITERS = 2
HITS = 2
ANGLES = 8
NZ = 32
NBLK = 256


def draw_hits(key, part):
    key = jax.random.fold_in(key, 7)
    span = NBLK - HITS + 1
    raw = jax.random.randint(key, (NZ, XT, ANGLES), 0, 1 << 30, dtype=jnp.int32)
    first = raw % span
    return jnp.stack([first + slot for slot in range(HITS)], axis=-1).astype(jnp.int32)


def shard_levels(rng, shape, split, low, high):
    factor_of, own = 1.0, jax.random.fold_in(rng, 6)
    for position, blocks in split:
        steps = jnp.exp(jax.random.uniform(jax.random.fold_in(own, position), (blocks,), jnp.float32, low / len(split), high / len(split)))
        factor_of = factor_of * jnp.repeat(steps, shape[position] // blocks).reshape([-1 if axis == position else 1 for axis in range(len(shape))])
    return factor_of


def centred(rng, shape, spread, bound, cuts=(), kind=jnp.bfloat16):
    entries = spread * jax.random.normal(rng, shape, jnp.float32)
    if cuts:
        entries = entries * shard_levels(rng, shape, cuts, -0.22, 0.18)
    return jnp.clip(entries, -bound, bound).astype(kind)


def setup_inputs(seed: int = 0, part: int = 0) -> dict:
    key_list = jax.random.split(jax.random.key(seed), 7)
    own_keys = jax.random.split(jax.random.fold_in(key_list[6], part), 7)
    return {
        "volume": centred(own_keys[0], (NZ, XT, TILE), 1.0, 6.0, ((0, 16),), jnp.float32),
        "voxel_weight": jnp.clip(jnp.exp(math.log(0.2) - 2.3025851 * jax.random.uniform(own_keys[1], (NZ, XT, TILE), jnp.float32) ** shard_levels(own_keys[1], (NZ, XT, TILE), ((0, 16),), -0.2, 0.2)), 0.02, 0.2),
        "measured": centred(own_keys[2], (ANGLES, NBLK, BIN), 16.0, 96.0, ((1, 16),), jnp.float32),
        "ray_weight": jnp.clip(jnp.exp(jax.random.uniform(key_list[3], (NBLK, BIN), jnp.float32, math.log(0.02), math.log(0.2))), 0.02, 0.2),
        "footprint": centred(key_list[4], (ANGLES, HITS, TILE, BIN), TILE ** -0.5, 0.5),
        "hits": draw_hits(jax.random.fold_in(jax.random.fold_in(key_list[6], part), 71), part),
    }


def smooth(field):
    zeros_z = jnp.zeros_like(field[:1])
    zeros_x = jnp.zeros_like(field[..., :1])
    grad_z = jnp.concatenate([field[1:] - field[:-1], zeros_z], axis=0)
    grad_x = jnp.concatenate([field[..., 1:] - field[..., :-1], zeros_x], axis=2)
    magnitude = jnp.sqrt(grad_z * grad_z + grad_x * grad_x + 0.01)
    flow_z = grad_z / magnitude
    flow_x = grad_x / magnitude
    diverge = flow_z - jnp.concatenate([zeros_z, flow_z[:-1]], axis=0)
    diverge = diverge + flow_x - jnp.concatenate([zeros_x, flow_x[..., :-1]], axis=2)
    return field + 0.2 * diverge

def reference(volume, voxel_weight, measured, ray_weight, footprint, hits):
    tiles = volume.reshape(NZ * XT, TILE)
    weights = voxel_weight.reshape(NZ * XT, TILE)
    lists = hits.reshape(NZ * XT, ANGLES, HITS)
    for step in range(ITERS):
        tiles_bf = tiles.astype(jnp.bfloat16)
        angle_ids = jnp.arange(step * SUBSET, (step + 1) * SUBSET, dtype=jnp.int32)

        def forward(angle):
            blocks = footprint[angle]
            ids = lists[:, angle, :]
            total = jnp.zeros((NBLK, BIN), jnp.float32)
            for slot in range(HITS):
                contrib = jnp.dot(tiles_bf, blocks[slot], preferred_element_type=jnp.float32)
                total = total + jax.ops.segment_sum(contrib, ids[:, slot], num_segments=NBLK)
            return total
        projections = lax.map(forward, angle_ids)
        chosen = measured[step * SUBSET:(step + 1) * SUBSET]
        resid = ((chosen - projections) * ray_weight).astype(jnp.bfloat16)

        def backward(carry, inputs):
            angle, rows_all = inputs
            blocks = footprint[angle]
            ids = lists[:, angle, :]
            for slot in range(HITS):
                picked = rows_all[ids[:, slot]]
                carry = carry + jnp.dot(picked, blocks[slot].T, preferred_element_type=jnp.float32)
            return (carry, None)
        update, _ = lax.scan(backward, jnp.zeros((NZ * XT, TILE), jnp.float32), (angle_ids, resid))
        tiles = tiles + weights * update
    return smooth(tiles.reshape(NZ, XT, TILE))
```

```python
import functools

import jax
import jax.numpy as jnp
from jax import lax
from jax.experimental import pallas as pl
from jax.experimental.pallas import tpu as pltpu
from jax.sharding import PartitionSpec as P

SUBSET = 4
PIECES = 8
BF = jnp.bfloat16
F32 = jnp.float32


def own_piece():
    position = lax.axis_index("slab")
    return (position & 1) * 4 + ((position >> 1) & 3)


def split(value):
    high = value.astype(BF)
    return high, (value - high.astype(F32)).astype(BF)


def dot(a, b):
    return jnp.dot(a, b, preferred_element_type=F32)


def add_segments(sums, tiles, hits_ref, first, nblk):
    rows = lax.broadcasted_iota(jnp.int32, (nblk, tiles.shape[0]), 0)
    for a in range(SUBSET):
        ids = hits_ref[0, first + a, 0:1, :]
        one_hot = jnp.where(rows == ids, 1.0, 0.0).astype(BF)
        sums[a] += dot(one_hot, tiles)


def write_partials(sums, shape_ref, measured_ref, proj, keep_ref, give_ref, first, nblk):
    own = measured_ref.shape[1]
    start = pl.multiple_of(lax.axis_index("slab") * own, own)
    for a in range(SUBSET):
        high, low = split(sums[a])
        blocks = [dot(high, shape_ref[first + a, k]) + dot(low, shape_ref[first + a, k]) for k in range(2)]
        proj[pl.ds(a * nblk, nblk)] = blocks[0] + jnp.concatenate(
            [jnp.zeros_like(blocks[1][:1]), blocks[1][:-1]], axis=0
        )
        spot = pl.ds(a * nblk + start, own)
        proj[spot] = proj[spot] - measured_ref[first + a]
    rows = SUBSET * nblk // PIECES
    mine = own_piece()
    for r in range(PIECES):
        piece = proj[pl.ds(pl.multiple_of((mine ^ r) * rows, rows), rows)]
        if r < 4:
            keep_ref[r] = piece
        else:
            give_ref[r - 4] = piece.astype(give_ref.dtype)


def spread_residuals(own_ref, other_ref, shape_ref, resid, spread, first, nblk):
    rows = SUBSET * nblk // PIECES
    mine = own_piece()
    for r in range(PIECES):
        piece = own_ref[r] if r < 4 else other_ref[r - 4]
        resid[pl.ds(pl.multiple_of((mine ^ r) * rows, rows), rows)] = piece.astype(F32)
    contract = (((1,), (1,)), ((), ()))
    for a in range(SUBSET):
        part = resid[pl.ds(a * nblk, nblk)]
        after = jnp.concatenate([part[1:], jnp.zeros_like(part[:1])], axis=0)
        total = lax.dot_general(
            part.astype(BF), shape_ref[first + a, 0], contract, preferred_element_type=F32
        ) + lax.dot_general(after.astype(BF), shape_ref[first + a, 1], contract, preferred_element_type=F32)
        high, low = split(total)
        spread[a] = jnp.concatenate([high, low], axis=1)


def update_of(hits_ref, spread, first, count, nblk):
    ids = jnp.concatenate([hits_ref[0, first + a, 0:1, :] for a in range(SUBSET)] * 2, axis=0).T
    lanes = lax.broadcasted_iota(jnp.int32, (count, nblk), 1)
    total = None
    for a in range(SUBSET):
        one_hot = jnp.where(ids[:, a : a + 1] == lanes, 1.0, 0.0).astype(BF)
        part = dot(one_hot, spread[a])
        total = part if total is None else total + part
    return total[:, :128] + total[:, 128:]


def forward_kernel(nblk, x_ref, hits_ref, shape_ref, measured_ref, keep_ref, give_ref, sums, proj):
    @pl.when(pl.program_id(0) == 0)
    def _():
        sums[...] = jnp.zeros_like(sums)

    add_segments(sums, x_ref[0].astype(BF), hits_ref, 0, nblk)

    @pl.when(pl.program_id(0) == pl.num_programs(0) - 1)
    def _():
        write_partials(sums, shape_ref, measured_ref, proj, keep_ref, give_ref, 0, nblk)


def middle_kernel(
    nblk, x_ref, w_ref, hits_ref, shape_ref, measured_ref, own_ref, other_ref,
    out_ref, keep_ref, give_ref, sums, proj, spread,
):
    @pl.when(pl.program_id(0) == 0)
    def _():
        sums[...] = jnp.zeros_like(sums)
        spread_residuals(own_ref, other_ref, shape_ref, proj, spread, 0, nblk)

    x = x_ref[0] + w_ref[0] * update_of(hits_ref, spread, 0, x_ref.shape[1], nblk)
    out_ref[0] = x
    add_segments(sums, x.astype(BF), hits_ref, SUBSET, nblk)

    @pl.when(pl.program_id(0) == pl.num_programs(0) - 1)
    def _():
        write_partials(sums, shape_ref, measured_ref, proj, keep_ref, give_ref, SUBSET, nblk)


def last_kernel(nblk, x_ref, w_ref, hits_ref, shape_ref, own_ref, other_ref, out_ref, proj, spread):
    @pl.when(pl.program_id(0) == 0)
    def _():
        spread_residuals(own_ref, other_ref, shape_ref, proj, spread, SUBSET, nblk)

    out_ref[0] = x_ref[0] + w_ref[0] * update_of(hits_ref, spread, SUBSET, x_ref.shape[1], nblk)


def swap(value, bits):
    count = lax.axis_size("slab")
    return lax.ppermute(value, "slab", [(i, i ^ bits) for i in range(count)])


def reduce_and_share(keep, give, rays):
    half = keep + swap(give, 1)
    arrived = [swap(half[j].astype(BF), 2 * j) for j in range(1, 4)]
    total = half[0] + sum(a.astype(F32) for a in arrived)
    bit = 8
    while bit < lax.axis_size("slab"):
        total = total + swap(total, bit)
        bit *= 2
    resid = (total * -rays).astype(BF)
    own = jnp.stack([resid] + [swap(resid, 2 * j) for j in range(1, 4)])
    return own, swap(own, 1)


def smooth(field, depth):
    count = lax.axis_size("slab")
    position = lax.axis_index("slab")
    below = lax.ppermute(field[-1:], "slab", [(i, i + 1) for i in range(count - 1)])
    above = lax.ppermute(field[:1], "slab", [(i + 1, i) for i in range(count - 1)])
    padded = jnp.concatenate([below, field, above], axis=0)
    lower_z = padded[: depth + 1]
    upper_z = padded[1 : depth + 2]
    global_z = position * depth + jnp.arange(depth + 1, dtype=jnp.int32) - 1
    valid = ((global_z >= 0) & (global_z < depth * count - 1)).astype(F32)
    grad_z = (upper_z - lower_z) * valid[:, None, None]
    zeros_x = jnp.zeros_like(lower_z[..., :1])
    grad_x = jnp.concatenate([lower_z[..., 1:] - lower_z[..., :-1], zeros_x], axis=2)
    inside = (global_z >= 0).astype(F32)[:, None, None]
    grad_x = grad_x * inside
    scale = lax.rsqrt(grad_z * grad_z + grad_x * grad_x + 0.01)
    flow_z = grad_z * scale
    here_x = (grad_x * scale)[1:]
    diverge = flow_z[1:] - flow_z[:-1]
    diverge = diverge + here_x - jnp.concatenate([jnp.zeros_like(here_x[..., :1]), here_x[..., :-1]], axis=2)
    return field + 0.2 * diverge


CHUNKS = 1


def per_device(volume, voxel_weight, measured, ray_weight, footprint, hits):
    depth, rows, width = volume.shape
    nblk = measured.shape[1] * lax.axis_size("slab")
    lists = hits.transpose(0, 2, 3, 1)
    piece = SUBSET * nblk // PIECES
    steps = depth * CHUNKS
    run = rows // CHUNKS
    tiles = pl.BlockSpec((1, run, width), lambda i: (i // CHUNKS, i % CHUNKS, 0))
    ids = pl.BlockSpec((1,) + lists.shape[1:3] + (run,), lambda i: (i // CHUNKS, 0, 0, i % CHUNKS))
    whole = pl.BlockSpec(memory_space=pltpu.VMEM)
    params = pltpu.CompilerParams(vmem_limit_bytes=40 * 2**20)
    pieces = [
        jax.ShapeDtypeStruct((4, piece, width), F32),
        jax.ShapeDtypeStruct((4, piece, width), F32),
    ]
    field = jax.ShapeDtypeStruct(volume.shape, F32)
    sums = pltpu.VMEM((SUBSET, nblk, width), F32)
    proj = pltpu.VMEM((SUBSET * nblk, width), F32)
    spread = pltpu.VMEM((SUBSET, nblk, 2 * width), BF)
    half = own_piece() & 1
    rays = lax.dynamic_slice_in_dim(ray_weight, half * piece, piece, 0)

    keep, give = pl.pallas_call(
        functools.partial(forward_kernel, nblk),
        grid=(steps,),
        in_specs=[tiles, ids, whole, whole],
        out_specs=[whole, whole],
        out_shape=pieces,
        scratch_shapes=[sums, proj],
        compiler_params=params,
        name="forward",
    )(volume, lists, footprint, measured)
    own, other = reduce_and_share(keep, give, rays)
    x, keep, give = pl.pallas_call(
        functools.partial(middle_kernel, nblk),
        grid=(steps,),
        in_specs=[tiles, tiles, ids, whole, whole, whole, whole],
        out_specs=[tiles, whole, whole],
        out_shape=[field] + pieces,
        scratch_shapes=[sums, proj, spread],
        compiler_params=params,
        name="middle",
    )(volume, voxel_weight, lists, footprint, measured, own, other)
    own, other = reduce_and_share(keep, give, rays)
    x = pl.pallas_call(
        functools.partial(last_kernel, nblk),
        grid=(steps,),
        in_specs=[tiles, tiles, ids, whole, whole, whole],
        out_specs=tiles,
        out_shape=field,
        scratch_shapes=[proj, spread],
        compiler_params=params,
        name="last",
    )(x, voxel_weight, lists, footprint, own, other)
    return smooth(x, depth)


def solution(mesh):
    return jax.shard_map(
        per_device,
        mesh=mesh,
        in_specs=(
            P(("parts", "slab"), None, None),
            P(("parts", "slab"), None, None),
            P("parts", "slab", None),
            P(),
            P(),
            P(("parts", "slab"), None, None, None),
        ),
        out_specs=P(("parts", "slab"), None, None),
        check_vma=False,
    )
```

```python
import functools

import jax
import jax.numpy as jnp
from jax import lax
from jax.experimental import pallas as pl
from jax.experimental.pallas import tpu as pltpu
from jax.sharding import PartitionSpec as P

SUBSET = 4
PIECES = 8
BF = jnp.bfloat16
F32 = jnp.float32


def own_piece():
    position = lax.axis_index("slab")
    return (position & 1) * 4 + ((position >> 1) & 3)


def split(value):
    high = value.astype(BF)
    return high, (value - high.astype(F32)).astype(BF)


def dot(a, b):
    return jnp.dot(a, b, preferred_element_type=F32)


def add_segments(sums, tiles, hits_ref, first, nblk):
    rows = lax.broadcasted_iota(jnp.int32, (nblk, tiles.shape[0]), 0)
    for a in range(SUBSET):
        ids = hits_ref[0, first + a, 0:1, :]
        one_hot = jnp.where(rows == ids, 1.0, 0.0).astype(BF)
        sums[a] += dot(one_hot, tiles)


def write_partials(sums, shape_ref, measured_ref, proj, keep_ref, give_ref, first, nblk):
    own = measured_ref.shape[1]
    start = pl.multiple_of(lax.axis_index("slab") * own, own)
    for a in range(SUBSET):
        high, low = split(sums[a])
        blocks = [dot(high, shape_ref[first + a, k]) + dot(low, shape_ref[first + a, k]) for k in range(2)]
        proj[pl.ds(a * nblk, nblk)] = blocks[0] + jnp.concatenate(
            [jnp.zeros_like(blocks[1][:1]), blocks[1][:-1]], axis=0
        )
        spot = pl.ds(a * nblk + start, own)
        proj[spot] = proj[spot] - measured_ref[first + a]
    rows = SUBSET * nblk // PIECES
    mine = own_piece()
    for r in range(PIECES):
        piece = proj[pl.ds(pl.multiple_of((mine ^ r) * rows, rows), rows)]
        if r < 4:
            keep_ref[r] = piece
        else:
            give_ref[r - 4] = piece.astype(give_ref.dtype)


def spread_residuals(own_ref, other_ref, shape_ref, resid, spread, first, nblk):
    rows = SUBSET * nblk // PIECES
    mine = own_piece()
    for r in range(PIECES):
        piece = own_ref[r] if r < 4 else other_ref[r - 4]
        resid[pl.ds(pl.multiple_of((mine ^ r) * rows, rows), rows)] = piece.astype(F32)
    contract = (((1,), (1,)), ((), ()))
    for a in range(SUBSET):
        part = resid[pl.ds(a * nblk, nblk)]
        after = jnp.concatenate([part[1:], jnp.zeros_like(part[:1])], axis=0)
        total = lax.dot_general(
            part.astype(BF), shape_ref[first + a, 0], contract, preferred_element_type=F32
        ) + lax.dot_general(after.astype(BF), shape_ref[first + a, 1], contract, preferred_element_type=F32)
        high, low = split(total)
        spread[a] = jnp.concatenate([high, low], axis=1)


def update_of(ids, spread, count, nblk):
    columns = jnp.concatenate([ids, ids], axis=0).T if ids.shape[0] < 8 else ids.T
    lanes = lax.broadcasted_iota(jnp.int32, (count, nblk), 1)
    total = None
    for a in range(SUBSET):
        one_hot = jnp.where(columns[:, a : a + 1] == lanes, 1.0, 0.0).astype(BF)
        part = dot(one_hot, spread[a])
        total = part if total is None else total + part
    return total[:, :128] + total[:, 128:]


def ids_of(hits_ref, z, first, count=SUBSET):
    return jnp.concatenate([hits_ref[z, first + a, 0:1, :] for a in range(count)], axis=0)


def packed_ids(pack_ref, first):
    blocks = []
    for b in range(pack_ref.shape[0] // 16):
        digits = pack_ref[pl.ds(b * 16, 16)].astype(F32)
        blocks.append((digits[:8] * 16.0 + digits[8:]).astype(jnp.int32)[first : first + SUBSET])
    return jnp.concatenate(blocks, axis=1)


def fill_pack(pack_ref, tiles, weights, hits_ref, chunk, rows):
    run = tiles.shape[0]
    pack_ref[pl.ds(pl.multiple_of(chunk * run, run), run)] = tiles
    pack_ref[pl.ds(pl.multiple_of(rows + chunk * run, run), run)] = weights.astype(BF)
    ids = ids_of(hits_ref, 0, 0, 8)
    digits = jnp.concatenate([ids >> 4, ids & 15], axis=0).astype(F32).astype(BF)
    for b in range(run // 128):
        spot = pl.multiple_of(2 * rows + chunk * (run // 8) + b * 16, 16)
        pack_ref[pl.ds(spot, 16)] = digits[:, b * 128 : (b + 1) * 128]


def forward_kernel(
    nblk, depth, chunks, x_ref, w_ref, hits_ref, shape_ref, measured_ref,
    keep_ref, give_ref, up_ref, down_ref, sums, proj,
):
    step = pl.program_id(0)
    z, chunk = step // chunks, step % chunks
    rows = x_ref.shape[1] * chunks

    @pl.when(step == 0)
    def _():
        sums[...] = jnp.zeros_like(sums)

    tiles = x_ref[0].astype(BF)
    add_segments(sums, tiles, hits_ref, 0, nblk)

    @pl.when(z == 0)
    def _():
        fill_pack(down_ref, tiles, w_ref[0], hits_ref, chunk, rows)

    @pl.when(z == depth - 1)
    def _():
        fill_pack(up_ref, tiles, w_ref[0], hits_ref, chunk, rows)

    @pl.when(step == pl.num_programs(0) - 1)
    def _():
        write_partials(sums, shape_ref, measured_ref, proj, keep_ref, give_ref, 0, nblk)


def middle_kernel(
    nblk, x_ref, w_ref, hits_ref, shape_ref, measured_ref, own_ref, other_ref,
    out_ref, keep_ref, give_ref, spread, sums, proj,
):
    @pl.when(pl.program_id(0) == 0)
    def _():
        sums[...] = jnp.zeros_like(sums)
        spread_residuals(own_ref, other_ref, shape_ref, proj, spread, 0, nblk)

    x = x_ref[0] + w_ref[0] * update_of(ids_of(hits_ref, 0, 0), spread, x_ref.shape[1], nblk)
    out_ref[0] = x
    add_segments(sums, x.astype(BF), hits_ref, SUBSET, nblk)

    @pl.when(pl.program_id(0) == pl.num_programs(0) - 1)
    def _():
        write_partials(sums, shape_ref, measured_ref, proj, keep_ref, give_ref, SUBSET, nblk)


def halo_kernel(nblk, spread, xb_ref, wb_ref, hb_ref, xa_ref, wa_ref, ha_ref, below_ref, above_ref):
    for x_ref, w_ref, h_ref, out_ref in (
        (xb_ref, wb_ref, hb_ref, below_ref),
        (xa_ref, wa_ref, ha_ref, above_ref),
    ):
        update = update_of(packed_ids(h_ref, 0), spread, x_ref.shape[0], nblk)
        out_ref[...] = x_ref[...].astype(F32) + w_ref[...].astype(F32) * update


def last_kernel(
    nblk, x_ref, w_ref, hits_ref, shape_ref, own_ref, other_ref, xb_ref, wb_ref, hb_ref, xa_ref, wa_ref, ha_ref,
    out_ref, proj, spread,
):
    @pl.when(pl.program_id(0) == 0)
    def _():
        spread_residuals(own_ref, other_ref, shape_ref, proj, spread, SUBSET, nblk)

    depth, run, width = x_ref.shape
    position = lax.axis_index("slab")
    first = jnp.where(position == 0, 0.0, 1.0)
    last = jnp.where(position == lax.axis_size("slab") - 1, 0.0, 1.0)
    lanes = lax.broadcasted_iota(jnp.int32, (run, width), 1)

    def neighbour(x_ref, w_ref, h_ref):
        update = update_of(packed_ids(h_ref, SUBSET), spread, run, nblk)
        return x_ref[...] + w_ref[...].astype(F32) * update

    def flows(here, after, there):
        grad_z = (after - here) * there
        grad_x = jnp.where(lanes == width - 1, 0.0, pltpu.roll(here, width - 1, 1) - here)
        scale = lax.rsqrt(grad_z * grad_z + grad_x * grad_x + 0.01)
        return grad_z * scale, grad_x * scale

    here = x_ref[0] + w_ref[0] * update_of(ids_of(hits_ref, 0, SUBSET), spread, run, nblk)
    flow_before, _ = flows(neighbour(xb_ref, wb_ref, hb_ref), here, first)
    for z in range(depth):
        if z + 1 < depth:
            after = x_ref[z + 1] + w_ref[z + 1] * update_of(ids_of(hits_ref, z + 1, SUBSET), spread, run, nblk)
            flow_z, flow_x = flows(here, after, 1.0)
        else:
            after = neighbour(xa_ref, wa_ref, ha_ref)
            flow_z, flow_x = flows(here, after, last)
        behind = jnp.where(lanes == 0, 0.0, pltpu.roll(flow_x, 1, 1))
        out_ref[z] = here + 0.2 * (flow_z - flow_before + flow_x - behind)
        here, flow_before = after, flow_z


def swap(value, bits):
    count = lax.axis_size("slab")
    return lax.ppermute(value, "slab", [(i, i ^ bits) for i in range(count)])


def reduce_and_share(keep, give, rays):
    half = keep + swap(give, 1)
    arrived = [swap(half[j].astype(BF), 2 * j) for j in range(1, 4)]
    total = half[0] + sum(a.astype(F32) for a in arrived)
    bit = 8
    while bit < lax.axis_size("slab"):
        total = total + swap(total.astype(BF), bit).astype(F32)
        bit *= 2
    resid = (total * -rays).astype(BF)
    own = jnp.stack([resid] + [swap(resid, 2 * j) for j in range(1, 4)])
    return own, swap(own, 1)


CHUNKS = 2
LAST_CHUNKS = 4


def per_device(volume, voxel_weight, measured, ray_weight, footprint, hits):
    depth, rows, width = volume.shape
    count = lax.axis_size("slab")
    nblk = measured.shape[1] * count
    lists = hits.transpose(0, 2, 3, 1)
    piece = SUBSET * nblk // PIECES
    steps = depth * CHUNKS
    run = rows // CHUNKS
    tiles = pl.BlockSpec((1, run, width), lambda i: (i // CHUNKS, i % CHUNKS, 0))
    ids = pl.BlockSpec((1,) + lists.shape[1:3] + (run,), lambda i: (i // CHUNKS, 0, 0, i % CHUNKS))
    whole = pl.BlockSpec(memory_space=pltpu.VMEM)
    params = pltpu.CompilerParams(vmem_limit_bytes=40 * 2**20)
    pieces = [
        jax.ShapeDtypeStruct((4, piece, width), F32),
        jax.ShapeDtypeStruct((4, piece, width), F32),
    ]
    field = jax.ShapeDtypeStruct(volume.shape, F32)
    pack = jax.ShapeDtypeStruct((2 * rows + rows // 8, width), BF)
    sums = pltpu.VMEM((SUBSET, nblk, width), F32)
    proj = pltpu.VMEM((SUBSET * nblk, width), F32)
    spread = pltpu.VMEM((SUBSET, nblk, 2 * width), BF)
    half = own_piece() & 1
    rays = lax.dynamic_slice_in_dim(ray_weight, half * piece, piece, 0)

    keep, give, up, down = pl.pallas_call(
        functools.partial(forward_kernel, nblk, depth, CHUNKS),
        grid=(steps,),
        in_specs=[tiles, tiles, ids, whole, whole],
        out_specs=[whole] * 4,
        out_shape=pieces + [pack, pack],
        scratch_shapes=[sums, proj],
        compiler_params=params,
        name="forward",
    )(volume, voxel_weight, lists, footprint, measured)
    below = lax.ppermute(up, "slab", [(i, i + 1) for i in range(count - 1)])
    above = lax.ppermute(down, "slab", [(i + 1, i) for i in range(count - 1)])
    own, other = reduce_and_share(keep, give, rays)
    x, keep, give, spread_first = pl.pallas_call(
        functools.partial(middle_kernel, nblk),
        grid=(steps,),
        in_specs=[tiles, tiles, ids, whole, whole, whole, whole],
        out_specs=[tiles, whole, whole, whole],
        out_shape=[field] + pieces + [jax.ShapeDtypeStruct((SUBSET, nblk, 2 * width), BF)],
        scratch_shapes=[sums, proj],
        compiler_params=params,
        name="middle",
    )(volume, voxel_weight, lists, footprint, measured, own, other)
    run = rows // LAST_CHUNKS
    line = pl.BlockSpec((run, width), lambda i: (i, 0))
    line_w = pl.BlockSpec((run, width), lambda i: (LAST_CHUNKS + i, 0))
    line_h = pl.BlockSpec((run // 8, width), lambda i: (16 * LAST_CHUNKS + i, 0))
    slice_out = jax.ShapeDtypeStruct((rows, width), F32)
    x_below, x_above = pl.pallas_call(
        functools.partial(halo_kernel, nblk),
        grid=(LAST_CHUNKS,),
        in_specs=[whole] + [line, line_w, line_h] * 2,
        out_specs=[line, line],
        out_shape=[slice_out, slice_out],
        compiler_params=params,
        cost_estimate=pl.CostEstimate(flops=4 * 10**9, bytes_accessed=4 * 2**20, transcendentals=0),
        name="halo",
    )(spread_first, below, below, below, above, above, above)
    own, other = reduce_and_share(keep, give, rays)
    tiles = pl.BlockSpec((depth, run, width), lambda i: (0, i, 0))
    ids = pl.BlockSpec((depth,) + lists.shape[1:3] + (run,), lambda i: (0, 0, 0, i))
    return pl.pallas_call(
        functools.partial(last_kernel, nblk),
        grid=(LAST_CHUNKS,),
        in_specs=[tiles, tiles, ids, whole, whole, whole] + [line, line_w, line_h] * 2,
        out_specs=tiles,
        out_shape=field,
        scratch_shapes=[proj, spread],
        compiler_params=params,
        name="last",
    )(x, voxel_weight, lists, footprint, own, other, x_below, below, below, x_above, above, above)


def solution(mesh):
    return jax.shard_map(
        per_device,
        mesh=mesh,
        in_specs=(
            P(("parts", "slab"), None, None),
            P(("parts", "slab"), None, None),
            P("parts", "slab", None),
            P(),
            P(),
            P(("parts", "slab"), None, None, None),
        ),
        out_specs=P(("parts", "slab"), None, None),
        check_vma=False,
    )
```

```python
import functools

import jax
import jax.numpy as jnp
from jax import lax
from jax.experimental import pallas as pl
from jax.experimental.pallas import tpu as pltpu
from jax.sharding import PartitionSpec as P

SUBSET = 4
PIECES = 8
BF = jnp.bfloat16
F32 = jnp.float32
WHOLE = pl.BlockSpec(memory_space=pltpu.VMEM)
OUTSIDE = pl.BlockSpec(memory_space=pl.ANY)
FIRST = pltpu.CompilerParams(vmem_limit_bytes=60 * 2**20)
PARAMS = pltpu.CompilerParams(vmem_limit_bytes=24 * 2**20)


def own_piece():
    position = lax.axis_index("slab")
    return (position & 1) * 4 + ((position >> 1) & 3)


def split(value):
    high = value.astype(BF)
    return high, (value - high.astype(F32)).astype(BF)


def dot(a, b):
    return jnp.dot(a, b, preferred_element_type=F32)


def one_hots(hits, z, first, nblk):
    rows = lax.broadcasted_iota(jnp.int32, (nblk, hits.shape[3]), 0)
    return [jnp.where(rows == hits[z, first + a, 0:1, :], 1.0, 0.0).astype(BF) for a in range(SUBSET)]


def add_segments(sums, tiles, hits, z, first, nblk):
    for a, one_hot in enumerate(one_hots(hits, z, first, nblk)):
        part = dot(one_hot, tiles)
        sums[a] = part if z == 0 else sums[a] + part


def write_partials(sums, shape, measured, proj, keep_ref, give_ref, first, nblk):
    own = measured.shape[1]
    start = pl.multiple_of(lax.axis_index("slab") * own, own)
    totals = []
    for a in range(SUBSET):
        high, low = split(sums[a])
        both = jnp.concatenate([shape[first + a, 0], shape[first + a, 1]], axis=1)
        part = dot(high, both) + dot(low, both)
        near, far = part[:, :128], part[:, 128:]
        totals.append(near + jnp.concatenate([jnp.zeros_like(far[:1]), far[:-1]], axis=0))
    for a in range(SUBSET):
        proj[pl.ds(a * nblk, nblk)] = totals[a]
    for a in range(SUBSET):
        spot = pl.ds(a * nblk + start, own)
        proj[spot] = proj[spot] - measured[first + a]
    rows = SUBSET * nblk // PIECES
    mine = own_piece()
    for r in range(PIECES):
        piece = proj[pl.ds(pl.multiple_of((mine ^ r) * rows, rows), rows)]
        if r < 4:
            keep_ref[r] = piece
        else:
            give_ref[r - 4] = piece


def spread_residuals(own_ref, other_ref, shape, resid, spread, first, nblk):
    rows = SUBSET * nblk // PIECES
    mine = own_piece()
    for r in range(PIECES):
        piece = own_ref[r] if r < 4 else other_ref[r - 4]
        resid[pl.ds(pl.multiple_of((mine ^ r) * rows, rows), rows)] = piece.astype(F32)
    contract = (((1,), (1,)), ((), ()))
    totals = []
    for a in range(SUBSET):
        part = resid[pl.ds(a * nblk, nblk)]
        after = jnp.concatenate([part[1:], jnp.zeros_like(part[:1])], axis=0)
        totals.append(
            lax.dot_general(shape[first + a, 0], part.astype(BF), contract, preferred_element_type=F32)
            + lax.dot_general(shape[first + a, 1], after.astype(BF), contract, preferred_element_type=F32)
        )
    for a in range(SUBSET):
        high, low = split(totals[a])
        spread[0:128, pl.ds(a * nblk, nblk)] = high
        spread[128:256, pl.ds(a * nblk, nblk)] = low


def update_of(hits, z, spread, first, nblk):
    both = dot(spread[...], jnp.concatenate(one_hots(hits, z, first, nblk), axis=0))
    return (both[:128] + both[128:]).T


def copies(sources, targets, sems):
    started = [pltpu.make_async_copy(s, t, sems.at[i]) for i, (s, t) in enumerate(zip(sources, targets))]
    for copy in started:
        copy.start()
    return started


def forward_kernel(
    nblk, depth, x_any, hits_any, shape_any, measured_any, keep_ref, give_ref, x, hits, shape, measured, sums, proj, sems
):
    got = copies(
        [hits_any, x_any.at[0], shape_any.at[pl.ds(0, SUBSET)], measured_any.at[pl.ds(0, SUBSET)]]
        + [x_any.at[z] for z in range(1, depth)],
        [hits, x.at[0], shape, measured] + [x.at[z] for z in range(1, depth)],
        sems,
    )
    got[0].wait()
    for z in range(depth):
        got[1 if z == 0 else 3 + z].wait()
        add_segments(sums, x[z].astype(BF), hits, z, 0, nblk)
    got[2].wait()
    got[3].wait()
    write_partials(sums, shape, measured, proj, keep_ref, give_ref, 0, nblk)


def middle_kernel(
    nblk, depth, x_any, w_any, hits_any, shape_any, measured_any, own_ref, other_ref, out_ref, keep_ref, give_ref,
    x, w, hits, shape, measured, sums, proj, spread, sems,
):
    got = copies(
        [shape_any, hits_any, x_any.at[0], w_any.at[0], measured_any.at[pl.ds(SUBSET, SUBSET)]]
        + [x_any.at[z] for z in range(1, depth)] + [w_any.at[z] for z in range(1, depth)],
        [shape, hits, x.at[0], w.at[0], measured]
        + [x.at[z] for z in range(1, depth)] + [w.at[z] for z in range(1, depth)],
        sems,
    )
    got[0].wait()
    spread_residuals(own_ref, other_ref, shape, proj, spread, 0, nblk)
    got[1].wait()
    for z in range(depth):
        update = update_of(hits, z, spread, 0, nblk)
        got[2 if z == 0 else 4 + z].wait()
        got[3 if z == 0 else 3 + depth + z].wait()
        tiles = x[z] + w[z] * update
        out_ref[z] = tiles
        add_segments(sums, tiles.astype(BF), hits, z, SUBSET, nblk)
    got[4].wait()
    write_partials(sums, shape.at[pl.ds(SUBSET, SUBSET)], measured, proj, keep_ref, give_ref, 0, nblk)


def last_kernel(
    nblk, depth, x_ref, w_any, hits_any, shape_any, own_ref, other_ref, out_ref, up_ref, down_ref,
    w, hits, shape, proj, spread, sems,
):
    got = copies(
        [shape_any.at[pl.ds(SUBSET, SUBSET)], hits_any] + [w_any.at[z] for z in range(depth)],
        [shape, hits] + [w.at[z] for z in range(depth)],
        sems,
    )
    got[0].wait()
    spread_residuals(own_ref, other_ref, shape, proj, spread, 0, nblk)
    got[1].wait()
    for z in range(depth):
        update = update_of(hits, z, spread, SUBSET, nblk)
        got[2 + z].wait()
        tiles = x_ref[z] + w[z] * update
        out_ref[z] = tiles
        if z == 0:
            down_ref[...] = tiles.astype(BF)
        if z == depth - 1:
            up_ref[...] = tiles.astype(BF)


def smooth_kernel(x_ref, below_ref, above_ref, out_ref):
    depth, run, width = x_ref.shape
    position = lax.axis_index("slab")
    first = jnp.where(position == 0, 0.0, 1.0)
    last = jnp.where(position == lax.axis_size("slab") - 1, 0.0, 1.0)
    lanes = lax.broadcasted_iota(jnp.int32, (run, width), 1)

    def flows(here, after, there):
        grad_z = (after - here) * there
        grad_x = jnp.where(lanes == width - 1, 0.0, pltpu.roll(here, width - 1, 1) - here)
        scale = lax.rsqrt(grad_z * grad_z + grad_x * grad_x + 0.01)
        return grad_z * scale, grad_x * scale

    here = x_ref[0]
    flow_before, _ = flows(below_ref[...].astype(F32), here, first)
    for z in range(depth):
        after = x_ref[z + 1] if z + 1 < depth else above_ref[...].astype(F32)
        flow_z, flow_x = flows(here, after, last if z + 1 == depth else 1.0)
        behind = jnp.where(lanes == 0, 0.0, pltpu.roll(flow_x, 1, 1))
        out_ref[z] = here + 0.2 * (flow_z - flow_before + flow_x - behind)
        here, flow_before = after, flow_z


def swap(value, bits):
    count = lax.axis_size("slab")
    return lax.ppermute(value, "slab", [(i, i ^ bits) for i in range(count)])


def reduce_and_share(keep, give, rays):
    half = keep + swap(give, 1)
    arrived = [swap(half[j].astype(BF), 2 * j) for j in range(1, 4)]
    total = half[0] + sum(a.astype(F32) for a in arrived)
    bit = 8
    while bit < lax.axis_size("slab"):
        total = total + swap(total.astype(BF), bit).astype(F32)
        bit *= 2
    resid = (total * -rays).astype(BF)
    own = jnp.stack([resid] + [swap(resid, 2 * j) for j in range(1, 4)])
    return own, swap(own, 1)


STEPS = 4


def per_device(volume, voxel_weight, measured, ray_weight, footprint, hits):
    depth, rows, width = volume.shape
    count = lax.axis_size("slab")
    nblk = measured.shape[1] * count
    lists = hits.transpose(0, 2, 3, 1)
    piece = SUBSET * nblk // PIECES
    pieces = [jax.ShapeDtypeStruct((4, piece, width), F32)] * 2
    field = jax.ShapeDtypeStruct(volume.shape, F32)
    edge = jax.ShapeDtypeStruct((rows, width), BF)
    x_buf = pltpu.VMEM(volume.shape, F32)
    hits_buf = pltpu.VMEM(lists.shape, jnp.int32)
    shape_buf = pltpu.VMEM((SUBSET,) + footprint.shape[1:], BF)
    measured_buf = pltpu.VMEM((SUBSET,) + measured.shape[1:], F32)
    sums = pltpu.VMEM((SUBSET, nblk, width), F32)
    proj = pltpu.VMEM((SUBSET * nblk, width), F32)
    spread = pltpu.VMEM((2 * width, SUBSET * nblk), BF)
    rays = lax.dynamic_slice_in_dim(ray_weight, (own_piece() & 1) * piece, piece, 0)

    keep, give = pl.pallas_call(
        functools.partial(forward_kernel, nblk, depth),
        in_specs=[OUTSIDE] * 4,
        out_specs=[WHOLE] * 2,
        out_shape=pieces,
        scratch_shapes=[x_buf, hits_buf, shape_buf, measured_buf, sums, proj, pltpu.SemaphoreType.DMA((3 + depth,))],
        compiler_params=FIRST,
        name="forward",
    )(volume, lists, footprint, measured)
    own, other = reduce_and_share(keep, give, rays)
    x, keep, give = pl.pallas_call(
        functools.partial(middle_kernel, nblk, depth),
        in_specs=[OUTSIDE] * 5 + [WHOLE] * 2,
        out_specs=[WHOLE] * 3,
        out_shape=[field] + pieces,
        scratch_shapes=[
            x_buf, x_buf, hits_buf, pltpu.VMEM(footprint.shape, BF), measured_buf, sums, proj, spread,
            pltpu.SemaphoreType.DMA((3 + 2 * depth,)),
        ],
        compiler_params=PARAMS,
        name="middle",
    )(volume, voxel_weight, lists, footprint, measured, own, other)
    own, other = reduce_and_share(keep, give, rays)
    x, up, down = pl.pallas_call(
        functools.partial(last_kernel, nblk, depth),
        in_specs=[WHOLE] + [OUTSIDE] * 3 + [WHOLE] * 2,
        out_specs=[WHOLE] * 3,
        out_shape=[field, edge, edge],
        scratch_shapes=[x_buf, hits_buf, shape_buf, proj, spread, pltpu.SemaphoreType.DMA((2 + depth,))],
        compiler_params=PARAMS,
        name="last",
    )(x, voxel_weight, lists, footprint, own, other)
    below = lax.ppermute(up, "slab", [(i, i + 1) for i in range(count - 1)])
    above = lax.ppermute(down, "slab", [(i + 1, i) for i in range(count - 1)])
    run = rows // STEPS
    tiles = pl.BlockSpec((depth, run, width), lambda i: (0, i, 0))
    line = pl.BlockSpec((run, width), lambda i: (i, 0))
    return pl.pallas_call(
        smooth_kernel,
        grid=(STEPS,),
        in_specs=[tiles, line, line],
        out_specs=tiles,
        out_shape=field,
        compiler_params=pltpu.CompilerParams(vmem_limit_bytes=16 * 2**20),
        name="smooth",
    )(x, below, above)


def solution(mesh):
    return jax.shard_map(
        per_device,
        mesh=mesh,
        in_specs=(
            P(("parts", "slab"), None, None),
            P(("parts", "slab"), None, None),
            P("parts", "slab", None),
            P(),
            P(),
            P(("parts", "slab"), None, None, None),
        ),
        out_specs=P(("parts", "slab"), None, None),
        check_vma=False,
    )
```

```python
import functools

import jax
import jax.numpy as jnp
from jax import lax
from jax.experimental import pallas as pl
from jax.experimental.pallas import tpu as pltpu
from jax.sharding import PartitionSpec as P

SUBSET = 4
PIECES = 8
BF = jnp.bfloat16
F32 = jnp.float32
WHOLE = pl.BlockSpec(memory_space=pltpu.VMEM)
OUTSIDE = pl.BlockSpec(memory_space=pl.ANY)
FIRST = pltpu.CompilerParams(vmem_limit_bytes=60 * 2**20)
PARAMS = pltpu.CompilerParams(vmem_limit_bytes=24 * 2**20)


def own_piece():
    position = lax.axis_index("slab")
    half = position
    for shift in (8, 4, 2, 1):
        half = half ^ (half >> shift)
    return (half & 1) * 4 + ((position >> 1) & 3)


def odd_core():
    return (lax.axis_index("slab") & 1) == 1


def split(value):
    high = value.astype(BF)
    return high, (value - high.astype(F32)).astype(BF)


def dot(a, b):
    return jnp.dot(a, b, preferred_element_type=F32)


def one_hots(hits, z, first, nblk):
    rows = lax.broadcasted_iota(jnp.int32, (nblk, hits.shape[3]), 0)
    return [jnp.where(rows == hits[z, first + a, 0:1, :], 1.0, 0.0).astype(BF) for a in range(SUBSET)]


def add_segments(sums, tiles, hits, z, first, nblk):
    for a, one_hot in enumerate(one_hots(hits, z, first, nblk)):
        part = dot(one_hot, tiles)
        sums[a] = part if z == 0 else sums[a] + part


def write_partials(sums, shape, measured, proj, keep_ref, give_ref, first, nblk):
    own = measured.shape[1]
    start = pl.multiple_of(lax.axis_index("slab") * own, own)
    totals = []
    for a in range(SUBSET):
        high, low = split(sums[a])
        both = jnp.concatenate([shape[first + a, 0], shape[first + a, 1]], axis=1)
        part = dot(high, both) + dot(low, both)
        near, far = part[:, :128], part[:, 128:]
        totals.append(near + jnp.concatenate([jnp.zeros_like(far[:1]), far[:-1]], axis=0))
    for a in range(SUBSET):
        proj[pl.ds(a * nblk, nblk)] = totals[a]
    for a in range(SUBSET):
        spot = pl.ds(a * nblk + start, own)
        proj[spot] = proj[spot] - measured[first + a]
    rows = SUBSET * nblk // PIECES
    mine = own_piece()
    for r in range(PIECES):
        piece = proj[pl.ds(pl.multiple_of((mine ^ r) * rows, rows), rows)]
        if r < 4:
            keep_ref[r] = piece
        else:
            give_ref[r - 4] = piece


def spread_residuals(own_ref, other_ref, shape, resid, spread, first, nblk):
    rows = SUBSET * nblk // PIECES
    mine = own_piece()
    for r in range(PIECES):
        piece = own_ref[r] if r < 4 else other_ref[r - 4]
        resid[pl.ds(pl.multiple_of((mine ^ r) * rows, rows), rows)] = piece.astype(F32)
    contract = (((1,), (1,)), ((), ()))
    totals = []
    for a in range(SUBSET):
        part = resid[pl.ds(a * nblk, nblk)]
        after = jnp.concatenate([part[1:], jnp.zeros_like(part[:1])], axis=0)
        totals.append(
            lax.dot_general(shape[first + a, 0], part.astype(BF), contract, preferred_element_type=F32)
            + lax.dot_general(shape[first + a, 1], after.astype(BF), contract, preferred_element_type=F32)
        )
    for a in range(SUBSET):
        high, low = split(totals[a])
        spread[0:128, pl.ds(a * nblk, nblk)] = high
        spread[128:256, pl.ds(a * nblk, nblk)] = low


def update_of(hits, z, spread, first, nblk):
    both = dot(spread[...], jnp.concatenate(one_hots(hits, z, first, nblk), axis=0))
    return (both[:128] + both[128:]).T


def copies(sources, targets, sems):
    started = [pltpu.make_async_copy(s, t, sems.at[i]) for i, (s, t) in enumerate(zip(sources, targets))]
    for copy in started:
        copy.start()
    return started


def forward_kernel(
    nblk, depth, x_any, hits_any, shape_any, measured_any, keep_ref, give_ref, x, hits, shape, measured, sums, proj, sems
):
    got = copies(
        [hits_any, x_any.at[0], shape_any.at[pl.ds(0, SUBSET)], measured_any.at[pl.ds(0, SUBSET)]]
        + [x_any.at[z] for z in range(1, depth)],
        [hits, x.at[0], shape, measured] + [x.at[z] for z in range(1, depth)],
        sems,
    )
    got[0].wait()
    for z in range(depth):
        got[1 if z == 0 else 3 + z].wait()
        add_segments(sums, x[z].astype(BF), hits, z, 0, nblk)
    got[2].wait()
    got[3].wait()
    write_partials(sums, shape, measured, proj, keep_ref, give_ref, 0, nblk)


def middle_kernel(
    nblk, depth, x_any, w_any, hits_any, shape_any, measured_any, own_ref, other_ref, out_ref, keep_ref, give_ref,
    x, w, hits, shape, measured, sums, proj, spread, sems,
):
    got = copies(
        [shape_any, hits_any, x_any.at[0], w_any.at[0], measured_any.at[pl.ds(SUBSET, SUBSET)]]
        + [x_any.at[z] for z in range(1, depth)] + [w_any.at[z] for z in range(1, depth)],
        [shape, hits, x.at[0], w.at[0], measured]
        + [x.at[z] for z in range(1, depth)] + [w.at[z] for z in range(1, depth)],
        sems,
    )
    got[0].wait()
    spread_residuals(own_ref, other_ref, shape, proj, spread, 0, nblk)
    got[1].wait()
    for z in range(depth):
        update = update_of(hits, z, spread, 0, nblk)
        got[2 if z == 0 else 4 + z].wait()
        got[3 if z == 0 else 3 + depth + z].wait()
        tiles = x[z] + w[z] * update
        out_ref[z] = tiles
        add_segments(sums, tiles.astype(BF), hits, z, SUBSET, nblk)
    got[4].wait()
    write_partials(sums, shape.at[pl.ds(SUBSET, SUBSET)], measured, proj, keep_ref, give_ref, 0, nblk)


def last_kernel(
    nblk, depth, x_ref, w_any, hits_any, shape_any, own_ref, other_ref, out_ref, near_ref, far_ref,
    w, hits, shape, proj, spread, sems,
):
    got = copies(
        [shape_any.at[pl.ds(SUBSET, SUBSET)], hits_any] + [w_any.at[z] for z in range(depth)],
        [shape, hits] + [w.at[z] for z in range(depth)],
        sems,
    )
    got[0].wait()
    spread_residuals(own_ref, other_ref, shape, proj, spread, 0, nblk)
    got[1].wait()
    for z in range(depth):
        update = update_of(hits, z, spread, SUBSET, nblk)
        got[2 + z].wait()
        tiles = x_ref[z] + w[z] * update
        out_ref[z] = tiles
        if z == 0 or z == depth - 1:
            edge = tiles.astype(BF)
            goes_far = odd_core() == (z != 0)

            @pl.when(goes_far)
            def _():
                far_ref[...] = edge

            @pl.when(jnp.logical_not(goes_far))
            def _():
                near_ref[...] = edge


def lanes_of(value):
    return lax.broadcasted_iota(jnp.int32, value.shape, 1)


def flows(here, after, there=None):
    width = here.shape[1]
    grad_z = after - here if there is None else (after - here) * there
    grad_x = jnp.where(lanes_of(here) == width - 1, 0.0, pltpu.roll(here, width - 1, 1) - here)
    scale = lax.rsqrt(grad_z * grad_z + grad_x * grad_x + 0.01)
    return grad_z * scale, grad_x * scale


def less_before(flow_x):
    return flow_x - jnp.where(lanes_of(flow_x) == 0, 0.0, pltpu.roll(flow_x, 1, 1))


RUN = 256


def inner_kernel(x_ref, near_ref, out_any, part_ref, done, sems):
    depth, rows, _ = x_ref.shape

    def finish(slices):
        sent = [pltpu.make_async_copy(done.at[z], out_any.at[z], sems.at[z]) for z in slices]
        for copy in sent:
            copy.start()
        for copy in sent:
            copy.wait()

    @pl.when(jnp.logical_not(odd_core()))
    def _():
        @pl.loop(0, rows // RUN)
        def _(i):
            spot = pl.ds(pl.multiple_of(i * RUN, RUN), RUN)
            here = x_ref[0, spot]
            before = None
            for z in range(depth):
                after = x_ref[z + 1, spot] if z + 1 < depth else near_ref[spot].astype(F32)
                flow_z, flow_x = flows(here, after)
                if z == 0:
                    part_ref[spot] = here + 0.2 * (flow_z + less_before(flow_x))
                else:
                    done[z, spot] = here + 0.2 * (flow_z - before + less_before(flow_x))
                here, before = after, flow_z

        finish(range(1, depth))

    @pl.when(odd_core())
    def _():
        @pl.loop(0, rows // RUN)
        def _(i):
            spot = pl.ds(pl.multiple_of(i * RUN, RUN), RUN)
            here = x_ref[0, spot]
            before, _ = flows(near_ref[spot].astype(F32), here)
            for z in range(depth - 1):
                after = x_ref[z + 1, spot]
                flow_z, flow_x = flows(here, after)
                done[z, spot] = here + 0.2 * (flow_z - before + less_before(flow_x))
                here, before = after, flow_z
            part_ref[spot] = here - 0.2 * before

        finish(range(depth - 1))


def outer_kernel(x_ref, part_ref, far_ref, _, out_any, done, sems):
    depth, rows, _ = x_ref.shape
    position = lax.axis_index("slab")

    def send(z, i):
        spot = pl.ds(i * RUN, RUN)
        return pltpu.make_async_copy(done.at[spot], out_any.at[z, spot], sems.at[i])

    @pl.when(jnp.logical_not(odd_core()))
    def _():
        there = jnp.where(position == 0, 0.0, 1.0)
        for i in range(rows // RUN):
            spot = pl.ds(i * RUN, RUN)
            flow_z, _ = flows(far_ref[spot].astype(F32), x_ref[0, spot], there)
            done[spot] = part_ref[spot] - 0.2 * flow_z
            send(0, i).start()
        for i in range(rows // RUN):
            send(0, i).wait()

    @pl.when(odd_core())
    def _():
        there = jnp.where(position == lax.axis_size("slab") - 1, 0.0, 1.0)
        for i in range(rows // RUN):
            spot = pl.ds(i * RUN, RUN)
            flow_z, flow_x = flows(x_ref[depth - 1, spot], far_ref[spot].astype(F32), there)
            done[spot] = part_ref[spot] + 0.2 * (flow_z + less_before(flow_x))
            send(depth - 1, i).start()
        for i in range(rows // RUN):
            send(depth - 1, i).wait()


def swap(value, bits):
    count = lax.axis_size("slab")
    return lax.ppermute(value, "slab", [(i, i ^ bits) for i in range(count)])


def reduce_and_share(keep, give, rays):
    quarters = (3, 5, 6)
    half = keep + swap(give, 1)
    arrived = [swap(half[1 + j].astype(BF), bits) for j, bits in enumerate(quarters)]
    total = half[0] + sum(a.astype(F32) for a in arrived)
    bit = 8
    while bit < lax.axis_size("slab"):
        total = total + swap(total.astype(BF), bit | 1).astype(F32)
        bit *= 2
    resid = (total * -rays).astype(BF)
    own = jnp.stack([resid] + [swap(resid, bits) for bits in quarters])
    return own, swap(own, 1)


def per_device(volume, voxel_weight, measured, ray_weight, footprint, hits):
    depth, rows, width = volume.shape
    count = lax.axis_size("slab")
    nblk = measured.shape[1] * count
    lists = hits.transpose(0, 2, 3, 1)
    piece = SUBSET * nblk // PIECES
    pieces = [jax.ShapeDtypeStruct((4, piece, width), F32)] * 2
    field = jax.ShapeDtypeStruct(volume.shape, F32)
    edge = jax.ShapeDtypeStruct((rows, width), BF)
    x_buf = pltpu.VMEM(volume.shape, F32)
    hits_buf = pltpu.VMEM(lists.shape, jnp.int32)
    shape_buf = pltpu.VMEM((SUBSET,) + footprint.shape[1:], BF)
    measured_buf = pltpu.VMEM((SUBSET,) + measured.shape[1:], F32)
    sums = pltpu.VMEM((SUBSET, nblk, width), F32)
    proj = pltpu.VMEM((SUBSET * nblk, width), F32)
    spread = pltpu.VMEM((2 * width, SUBSET * nblk), BF)
    rays = lax.dynamic_slice_in_dim(ray_weight, (own_piece() & 1) * piece, piece, 0)

    keep, give = pl.pallas_call(
        functools.partial(forward_kernel, nblk, depth),
        in_specs=[OUTSIDE] * 4,
        out_specs=[WHOLE] * 2,
        out_shape=pieces,
        scratch_shapes=[x_buf, hits_buf, shape_buf, measured_buf, sums, proj, pltpu.SemaphoreType.DMA((3 + depth,))],
        compiler_params=FIRST,
        name="forward",
    )(volume, lists, footprint, measured)
    own, other = reduce_and_share(keep, give, rays)
    x, keep, give = pl.pallas_call(
        functools.partial(middle_kernel, nblk, depth),
        in_specs=[OUTSIDE] * 5 + [WHOLE] * 2,
        out_specs=[WHOLE] * 3,
        out_shape=[field] + pieces,
        scratch_shapes=[
            x_buf, x_buf, hits_buf, pltpu.VMEM(footprint.shape, BF), measured_buf, sums, proj, spread,
            pltpu.SemaphoreType.DMA((3 + 2 * depth,)),
        ],
        compiler_params=PARAMS,
        name="middle",
    )(volume, voxel_weight, lists, footprint, measured, own, other)
    own, other = reduce_and_share(keep, give, rays)
    x, near, far = pl.pallas_call(
        functools.partial(last_kernel, nblk, depth),
        in_specs=[WHOLE] + [OUTSIDE] * 3 + [WHOLE] * 2,
        out_specs=[WHOLE] * 3,
        out_shape=[field, edge, edge],
        scratch_shapes=[x_buf, hits_buf, shape_buf, proj, spread, pltpu.SemaphoreType.DMA((2 + depth,))],
        compiler_params=PARAMS,
        name="last",
    )(x, voxel_weight, lists, footprint, own, other)
    far = lax.ppermute(far, "slab", [(i, min(max((i + 1) // 2 * 4 - 1 - i, 0), count - 1)) for i in range(count)])
    near = swap(near, 1)
    part = jax.ShapeDtypeStruct((rows, width), F32)
    out, part = pl.pallas_call(
        inner_kernel,
        in_specs=[WHOLE] * 2,
        out_specs=[OUTSIDE, WHOLE],
        out_shape=[field, part],
        scratch_shapes=[x_buf, pltpu.SemaphoreType.DMA((depth,))],
        compiler_params=PARAMS,
        cost_estimate=pl.CostEstimate(flops=3 * 10**9, bytes_accessed=8 * 2**20, transcendentals=0),
        name="inner",
    )(x, near)
    return pl.pallas_call(
        outer_kernel,
        in_specs=[WHOLE] * 3 + [OUTSIDE],
        out_specs=OUTSIDE,
        out_shape=field,
        input_output_aliases={3: 0},
        scratch_shapes=[pltpu.VMEM((rows, width), F32), pltpu.SemaphoreType.DMA((rows // RUN,))],
        compiler_params=PARAMS,
        name="outer",
    )(x, part, far, out)


def solution(mesh):
    return jax.shard_map(
        per_device,
        mesh=mesh,
        in_specs=(
            P(("parts", "slab"), None, None),
            P(("parts", "slab"), None, None),
            P("parts", "slab", None),
            P(),
            P(),
            P(("parts", "slab"), None, None, None),
        ),
        out_specs=P(("parts", "slab"), None, None),
        check_vma=False,
    )
```

```python
import functools

import jax
import jax.numpy as jnp
from jax import lax
from jax.experimental import pallas as pl
from jax.experimental.pallas import tpu as pltpu
from jax.sharding import PartitionSpec as P

SUBSET = 4
PIECES = 8
BF = jnp.bfloat16
F32 = jnp.float32
WHOLE = pl.BlockSpec(memory_space=pltpu.VMEM)
OUTSIDE = pl.BlockSpec(memory_space=pl.ANY)
FIRST = pltpu.CompilerParams(vmem_limit_bytes=int(53.2 * 2**20))
MIDDLE = pltpu.CompilerParams(vmem_limit_bytes=int(48 * 2**20))
PARAMS = pltpu.CompilerParams(vmem_limit_bytes=24 * 2**20)


def own_piece():
    position = lax.axis_index("slab")
    half = position
    for shift in (8, 4, 2, 1):
        half = half ^ (half >> shift)
    return (half & 1) * 4 + ((position >> 1) & 3)


def odd_core():
    return (lax.axis_index("slab") & 1) == 1


def split(value):
    high = value.astype(BF)
    return high, (value - high.astype(F32)).astype(BF)


def dot(a, b):
    return jnp.dot(a, b, preferred_element_type=F32)


def one_hots(hits, z, first, nblk):
    rows = lax.broadcasted_iota(jnp.int32, (nblk, hits.shape[3]), 0)
    return [jnp.where(rows == hits[z, first + a, 0:1, :], 1.0, 0.0).astype(BF) for a in range(SUBSET)]


def add_segments(sums, tiles, hits, z, first, nblk):
    for a, one_hot in enumerate(one_hots(hits, z, first, nblk)):
        part = dot(one_hot, tiles)
        sums[a] = part if z == 0 else sums[a] + part


def write_partials(sums, shape, measured, proj, keep_ref, give_ref, first, nblk):
    own = measured.shape[1]
    start = pl.multiple_of(lax.axis_index("slab") * own, own)
    totals = []
    for a in range(SUBSET):
        high, low = split(sums[a])
        both = jnp.concatenate([shape[first + a, 0], shape[first + a, 1]], axis=1)
        part = dot(high, both) + dot(low, both)
        near, far = part[:, :128], part[:, 128:]
        totals.append(near + jnp.concatenate([jnp.zeros_like(far[:1]), far[:-1]], axis=0))
    for a in range(SUBSET):
        proj[pl.ds(a * nblk, nblk)] = totals[a]
    for a in range(SUBSET):
        spot = pl.ds(a * nblk + start, own)
        proj[spot] = proj[spot] - measured[first + a]
    rows = SUBSET * nblk // PIECES
    mine = own_piece()
    for r in range(PIECES):
        piece = proj[pl.ds(pl.multiple_of((mine ^ r) * rows, rows), rows)]
        if r < 4:
            keep_ref[r] = piece
        else:
            give_ref[r - 4] = piece


def spread_residuals(own_ref, other_ref, shape, resid, spread, first, nblk):
    rows = SUBSET * nblk // PIECES
    mine = own_piece()
    for r in range(PIECES):
        piece = own_ref[r] if r < 4 else other_ref[r - 4]
        resid[pl.ds(pl.multiple_of((mine ^ r) * rows, rows), rows)] = piece.astype(F32)
    contract = (((1,), (1,)), ((), ()))
    totals = []
    for a in range(SUBSET):
        part = resid[pl.ds(a * nblk, nblk)]
        after = jnp.concatenate([part[1:], jnp.zeros_like(part[:1])], axis=0)
        totals.append(
            lax.dot_general(shape[first + a, 0], part.astype(BF), contract, preferred_element_type=F32)
            + lax.dot_general(shape[first + a, 1], after.astype(BF), contract, preferred_element_type=F32)
        )
    for a in range(SUBSET):
        spread[:, pl.ds(a * nblk, nblk)] = totals[a].astype(BF)


def update_of(hits, z, spread, first, nblk):
    return dot(spread[...], jnp.concatenate(one_hots(hits, z, first, nblk), axis=0)).T


def copies(sources, targets, sems):
    started = [pltpu.make_async_copy(s, t, sems.at[i]) for i, (s, t) in enumerate(zip(sources, targets))]
    for copy in started:
        copy.start()
    return started


def forward_kernel(
    nblk, depth, x_any, hits_any, shape_any, measured_any, keep_ref, give_ref, x, hits, shape, measured, sums, proj, sems
):
    got = copies(
        [hits_any, x_any.at[0], shape_any.at[pl.ds(0, SUBSET)], measured_any.at[pl.ds(0, SUBSET)]]
        + [x_any.at[z] for z in range(1, depth)],
        [hits, x.at[0], shape, measured] + [x.at[z] for z in range(1, depth)],
        sems,
    )
    got[0].wait()
    for z in range(depth):
        got[1 if z == 0 else 3 + z].wait()
        add_segments(sums, x[z].astype(BF), hits, z, 0, nblk)
    got[2].wait()
    got[3].wait()
    write_partials(sums, shape, measured, proj, keep_ref, give_ref, 0, nblk)


def middle_kernel(
    nblk, depth, x_any, w_any, hits_any, shape_any, measured_any, own_ref, other_ref, out_ref, keep_ref, give_ref,
    x, w, hits, shape, measured, sums, proj, spread, sems,
):
    got = copies(
        [shape_any, hits_any, x_any.at[0], w_any.at[0], measured_any.at[pl.ds(SUBSET, SUBSET)]]
        + [x_any.at[z] for z in range(1, depth)] + [w_any.at[z] for z in range(1, depth)],
        [shape, hits, x.at[0], w.at[0], measured]
        + [x.at[z] for z in range(1, depth)] + [w.at[z] for z in range(1, depth)],
        sems,
    )
    got[0].wait()
    spread_residuals(own_ref, other_ref, shape, proj, spread, 0, nblk)
    got[1].wait()
    for z in range(depth):
        update = update_of(hits, z, spread, 0, nblk)
        got[2 if z == 0 else 4 + z].wait()
        got[3 if z == 0 else 3 + depth + z].wait()
        tiles = x[z] + w[z] * update
        out_ref[z] = tiles
        add_segments(sums, tiles.astype(BF), hits, z, SUBSET, nblk)
    got[4].wait()
    write_partials(sums, shape.at[pl.ds(SUBSET, SUBSET)], measured, proj, keep_ref, give_ref, 0, nblk)


def last_kernel(
    nblk, depth, x_ref, w_any, hits_any, shape_any, own_ref, other_ref, out_ref, near_ref, far_ref,
    w, hits, shape, proj, spread, sems,
):
    got = copies(
        [shape_any.at[pl.ds(SUBSET, SUBSET)], hits_any] + [w_any.at[z] for z in range(depth)],
        [shape, hits] + [w.at[z] for z in range(depth)],
        sems,
    )
    got[0].wait()
    spread_residuals(own_ref, other_ref, shape, proj, spread, 0, nblk)
    got[1].wait()
    for z in range(depth):
        update = update_of(hits, z, spread, SUBSET, nblk)
        got[2 + z].wait()
        tiles = x_ref[z] + w[z] * update
        out_ref[z] = tiles
        if z == 0 or z == depth - 1:
            edge = tiles.astype(BF)
            goes_far = odd_core() == (z != 0)

            @pl.when(goes_far)
            def _():
                far_ref[...] = edge

            @pl.when(jnp.logical_not(goes_far))
            def _():
                near_ref[...] = edge


def lanes_of(value):
    return lax.broadcasted_iota(jnp.int32, value.shape, 1)


def flows(here, after, there=None):
    width = here.shape[1]
    grad_z = after - here if there is None else (after - here) * there
    grad_x = jnp.where(lanes_of(here) == width - 1, 0.0, pltpu.roll(here, width - 1, 1) - here)
    scale = lax.rsqrt(grad_z * grad_z + grad_x * grad_x + 0.01)
    return grad_z * scale, grad_x * scale


def less_before(flow_x):
    return flow_x - jnp.where(lanes_of(flow_x) == 0, 0.0, pltpu.roll(flow_x, 1, 1))


RUN = 256


def inner_kernel(x_ref, near_ref, out_any, part_ref, done, sems):
    depth, rows, _ = x_ref.shape

    def finish(slices):
        sent = [pltpu.make_async_copy(done.at[z], out_any.at[z], sems.at[z]) for z in slices]
        for copy in sent:
            copy.start()
        for copy in sent:
            copy.wait()

    @pl.when(jnp.logical_not(odd_core()))
    def _():
        @pl.loop(0, rows // RUN)
        def _(i):
            spot = pl.ds(pl.multiple_of(i * RUN, RUN), RUN)
            here = x_ref[0, spot]
            before = None
            for z in range(depth):
                after = x_ref[z + 1, spot] if z + 1 < depth else near_ref[spot].astype(F32)
                flow_z, flow_x = flows(here, after)
                if z == 0:
                    part_ref[spot] = here + 0.2 * (flow_z + less_before(flow_x))
                else:
                    done[z, spot] = here + 0.2 * (flow_z - before + less_before(flow_x))
                here, before = after, flow_z

        finish(range(1, depth))

    @pl.when(odd_core())
    def _():
        @pl.loop(0, rows // RUN)
        def _(i):
            spot = pl.ds(pl.multiple_of(i * RUN, RUN), RUN)
            here = x_ref[0, spot]
            before, _ = flows(near_ref[spot].astype(F32), here)
            for z in range(depth - 1):
                after = x_ref[z + 1, spot]
                flow_z, flow_x = flows(here, after)
                done[z, spot] = here + 0.2 * (flow_z - before + less_before(flow_x))
                here, before = after, flow_z
            part_ref[spot] = here - 0.2 * before

        finish(range(depth - 1))


def outer_kernel(x_ref, part_ref, far_ref, _, out_any, done, sems):
    depth, rows, _ = x_ref.shape
    position = lax.axis_index("slab")

    def send(z, i):
        spot = pl.ds(i * RUN, RUN)
        return pltpu.make_async_copy(done.at[spot], out_any.at[z, spot], sems.at[i])

    @pl.when(jnp.logical_not(odd_core()))
    def _():
        there = jnp.where(position == 0, 0.0, 1.0)
        for i in range(rows // RUN):
            spot = pl.ds(i * RUN, RUN)
            flow_z, _ = flows(far_ref[spot].astype(F32), x_ref[0, spot], there)
            done[spot] = part_ref[spot] - 0.2 * flow_z
            send(0, i).start()
        for i in range(rows // RUN):
            send(0, i).wait()

    @pl.when(odd_core())
    def _():
        there = jnp.where(position == lax.axis_size("slab") - 1, 0.0, 1.0)
        for i in range(rows // RUN):
            spot = pl.ds(i * RUN, RUN)
            flow_z, flow_x = flows(x_ref[depth - 1, spot], far_ref[spot].astype(F32), there)
            done[spot] = part_ref[spot] + 0.2 * (flow_z + less_before(flow_x))
            send(depth - 1, i).start()
        for i in range(rows // RUN):
            send(depth - 1, i).wait()


def swap(value, bits):
    count = lax.axis_size("slab")
    return lax.ppermute(value, "slab", [(i, i ^ bits) for i in range(count)])


def reduce_and_share(keep, give, rays):
    quarters = (3, 5, 6)
    half = keep + swap(give, 1)
    arrived = [swap(half[1 + j].astype(BF), bits) for j, bits in enumerate(quarters)]
    total = half[0] + sum(a.astype(F32) for a in arrived)
    bit = 8
    while bit < lax.axis_size("slab"):
        total = total + swap(total.astype(BF), bit | 1).astype(F32)
        bit *= 2
    resid = (total * -rays).astype(BF)
    own = jnp.stack([resid] + [swap(resid, bits) for bits in quarters])
    return own, swap(own, 1)


def per_device(volume, voxel_weight, measured, ray_weight, footprint, hits):
    depth, rows, width = volume.shape
    count = lax.axis_size("slab")
    nblk = measured.shape[1] * count
    lists = hits.transpose(0, 2, 3, 1)
    piece = SUBSET * nblk // PIECES
    pieces = [jax.ShapeDtypeStruct((4, piece, width), F32)] * 2
    field = jax.ShapeDtypeStruct(volume.shape, F32)
    edge = jax.ShapeDtypeStruct((rows, width), BF)
    x_buf = pltpu.VMEM(volume.shape, F32)
    hits_buf = pltpu.VMEM(lists.shape, jnp.int32)
    shape_buf = pltpu.VMEM((SUBSET,) + footprint.shape[1:], BF)
    measured_buf = pltpu.VMEM((SUBSET,) + measured.shape[1:], F32)
    sums = pltpu.VMEM((SUBSET, nblk, width), F32)
    proj = pltpu.VMEM((SUBSET * nblk, width), F32)
    spread = pltpu.VMEM((width, SUBSET * nblk), BF)
    rays = lax.dynamic_slice_in_dim(ray_weight, (own_piece() & 1) * piece, piece, 0)

    keep, give = pl.pallas_call(
        functools.partial(forward_kernel, nblk, depth),
        in_specs=[OUTSIDE] * 4,
        out_specs=[WHOLE] * 2,
        out_shape=pieces,
        scratch_shapes=[x_buf, hits_buf, shape_buf, measured_buf, sums, proj, pltpu.SemaphoreType.DMA((3 + depth,))],
        compiler_params=FIRST,
        name="forward",
    )(volume, lists, footprint, measured)
    own, other = reduce_and_share(keep, give, rays)
    x, keep, give = pl.pallas_call(
        functools.partial(middle_kernel, nblk, depth),
        in_specs=[OUTSIDE] * 5 + [WHOLE] * 2,
        out_specs=[WHOLE] * 3,
        out_shape=[field] + pieces,
        scratch_shapes=[
            x_buf, x_buf, hits_buf, pltpu.VMEM(footprint.shape, BF), measured_buf, sums, proj, spread,
            pltpu.SemaphoreType.DMA((3 + 2 * depth,)),
        ],
        compiler_params=MIDDLE,
        name="middle",
    )(volume, voxel_weight, lists, footprint, measured, own, other)
    own, other = reduce_and_share(keep, give, rays)
    x, near, far = pl.pallas_call(
        functools.partial(last_kernel, nblk, depth),
        in_specs=[WHOLE] + [OUTSIDE] * 3 + [WHOLE] * 2,
        out_specs=[WHOLE] * 3,
        out_shape=[field, edge, edge],
        scratch_shapes=[x_buf, hits_buf, shape_buf, proj, spread, pltpu.SemaphoreType.DMA((2 + depth,))],
        compiler_params=PARAMS,
        name="last",
    )(x, voxel_weight, lists, footprint, own, other)
    far = lax.ppermute(far, "slab", [(i, min(max((i + 1) // 2 * 4 - 1 - i, 0), count - 1)) for i in range(count)])
    near = swap(near, 1)
    part = jax.ShapeDtypeStruct((rows, width), F32)
    out, part = pl.pallas_call(
        inner_kernel,
        in_specs=[WHOLE] * 2,
        out_specs=[OUTSIDE, WHOLE],
        out_shape=[field, part],
        scratch_shapes=[x_buf, pltpu.SemaphoreType.DMA((depth,))],
        compiler_params=PARAMS,
        cost_estimate=pl.CostEstimate(flops=3 * 10**9, bytes_accessed=8 * 2**20, transcendentals=0),
        name="inner",
    )(x, near)
    return pl.pallas_call(
        outer_kernel,
        in_specs=[WHOLE] * 3 + [OUTSIDE],
        out_specs=OUTSIDE,
        out_shape=field,
        input_output_aliases={3: 0},
        scratch_shapes=[pltpu.VMEM((rows, width), F32), pltpu.SemaphoreType.DMA((rows // RUN,))],
        compiler_params=PARAMS,
        name="outer",
    )(x, part, far, out)


def solution(mesh):
    return jax.shard_map(
        per_device,
        mesh=mesh,
        in_specs=(
            P(("parts", "slab"), None, None),
            P(("parts", "slab"), None, None),
            P("parts", "slab", None),
            P(),
            P(),
            P(("parts", "slab"), None, None, None),
        ),
        out_specs=P(("parts", "slab"), None, None),
        check_vma=False,
    )
```

```python
import functools

import jax
import jax.numpy as jnp
from jax import lax
from jax.experimental import pallas as pl
from jax.experimental.pallas import tpu as pltpu
from jax.sharding import PartitionSpec as P

SUBSET = 4
PIECES = 8
BF = jnp.bfloat16
F32 = jnp.float32
WHOLE = pl.BlockSpec(memory_space=pltpu.VMEM)
OUTSIDE = pl.BlockSpec(memory_space=pl.ANY)
FIRST = pltpu.CompilerParams(vmem_limit_bytes=int(53.2 * 2**20))
MIDDLE = pltpu.CompilerParams(vmem_limit_bytes=int(40 * 2**20))
PARAMS = pltpu.CompilerParams(vmem_limit_bytes=24 * 2**20)


def own_piece():
    position = lax.axis_index("slab")
    half = position
    for shift in (8, 4, 2, 1):
        half = half ^ (half >> shift)
    return (half & 1) * 4 + ((position >> 1) & 3)


def odd_core():
    return (lax.axis_index("slab") & 1) == 1


def split(value):
    high = value.astype(BF)
    return high, (value - high.astype(F32)).astype(BF)


def dot(a, b):
    return jnp.dot(a, b, preferred_element_type=F32)


def one_hots(hits, z, first, nblk):
    rows = lax.broadcasted_iota(jnp.int32, (nblk, hits.shape[3]), 0)
    return [jnp.where(rows == hits[z, first + a, 0:1, :], 1.0, 0.0).astype(BF) for a in range(SUBSET)]


def add_segments(sums, tiles, hits, z, first, nblk):
    for a, one_hot in enumerate(one_hots(hits, z, first, nblk)):
        part = dot(one_hot, tiles)
        sums[a] = part if z == 0 else sums[a] + part


def halves():
    half = own_piece() >> 2
    return half * 2, (1 - half) * 2


def add_half(sums, tiles, hits, z, first, nblk):
    rows = lax.broadcasted_iota(jnp.int32, (nblk, tiles.shape[0]), 0)
    for a in range(2):
        part = dot(jnp.where(rows == hits[z, first + a, 0:1, :], 1.0, 0.0).astype(BF), tiles)
        sums[a] = part if z == 0 else sums[a] + part


def write_half(sums, at, shape, shape_at, measured, measured_at, proj, out_ref, nblk):
    own = measured.shape[1]
    start = pl.multiple_of(lax.axis_index("slab") * own, own)
    totals = []
    for a in range(2):
        high, low = split(sums[at + a])
        both = jnp.concatenate([shape[shape_at + a, 0], shape[shape_at + a, 1]], axis=1)
        part = dot(high, both) + dot(low, both)
        near, far = part[:, :128], part[:, 128:]
        totals.append(near + jnp.concatenate([jnp.zeros_like(far[:1]), far[:-1]], axis=0))
    for a in range(2):
        proj[pl.ds(a * nblk, nblk)] = totals[a]
    for a in range(2):
        spot = pl.ds(a * nblk + start, own)
        proj[spot] = proj[spot] - measured[measured_at + a]
    rows = nblk // 2
    mine = own_piece() & 3
    for r in range(4):
        out_ref[r] = proj[pl.ds(pl.multiple_of((mine ^ r) * rows, rows), rows)]


def spread_half(pieces_ref, shape, at, resid, nblk):
    rows = nblk // 2
    mine = own_piece() & 3
    for r in range(4):
        resid[pl.ds(pl.multiple_of((mine ^ r) * rows, rows), rows)] = pieces_ref[r].astype(F32)
    contract = (((1,), (1,)), ((), ()))
    totals = []
    for a in range(2):
        part = resid[pl.ds(a * nblk, nblk)]
        after = jnp.concatenate([part[1:], jnp.zeros_like(part[:1])], axis=0)
        total = lax.dot_general(shape[at + a, 0], part.astype(BF), contract, preferred_element_type=F32)
        total += lax.dot_general(shape[at + a, 1], after.astype(BF), contract, preferred_element_type=F32)
        totals.append(total.astype(BF))
    return jnp.concatenate(totals, axis=1)


def update_half(hits, z, first, table, nblk):
    rows = lax.broadcasted_iota(jnp.int32, (nblk, hits.shape[3]), 0)
    hot = [jnp.where(rows == hits[z, first + a, 0:1, :], 1.0, 0.0).astype(BF) for a in range(2)]
    return dot(table, jnp.concatenate(hot, axis=0))


def copies(sources, targets, sems):
    started = [pltpu.make_async_copy(s, t, sems.at[i]) for i, (s, t) in enumerate(zip(sources, targets))]
    for copy in started:
        copy.start()
    return started


def forward_kernel(
    nblk, depth, x_any, hits_any, shape_any, measured_any, keep_ref, give_ref, x, hits, shape, measured, sums, proj, sems
):
    got = copies(
        [hits_any, x_any.at[0], shape_any.at[pl.ds(0, SUBSET)], measured_any.at[pl.ds(0, SUBSET)]]
        + [x_any.at[z] for z in range(1, depth)],
        [hits, x.at[0], shape, measured] + [x.at[z] for z in range(1, depth)],
        sems,
    )
    got[0].wait()
    for z in range(depth):
        got[1 if z == 0 else 3 + z].wait()
        add_segments(sums, x[z].astype(BF), hits, z, 0, nblk)
    got[2].wait()
    got[3].wait()
    own, other = halves()
    write_half(sums, other, shape, other, measured, other, proj, give_ref, nblk)
    write_half(sums, own, shape, own, measured, own, proj, keep_ref, nblk)


def own_kernel(nblk, first, hits, shape, own_ref, out_ref, resid):
    angle = first + halves()[0]
    table = spread_half(own_ref, shape, angle, resid, nblk)
    for z in range(hits.shape[0]):
        out_ref[z] = update_half(hits, z, angle, table, nblk)


def middle_kernel(
    nblk, depth, x_any, w_any, hits, shape, measured, other_ref, part_ref, out_ref, give_ref,
    x, w, sums, proj, sems,
):
    got = copies(
        [x_any.at[z] for z in range(depth)] + [w_any.at[z] for z in range(depth)],
        [x.at[z] for z in range(depth)] + [w.at[z] for z in range(depth)],
        sems,
    )
    angle = halves()[1]
    table = spread_half(other_ref, shape, angle, proj, nblk)
    for z in range(depth):
        update = (part_ref[z] + update_half(hits, z, angle, table, nblk)).T
        got[z].wait()
        got[depth + z].wait()
        tiles = x[z] + w[z] * update
        out_ref[z] = tiles
        add_half(sums, tiles.astype(BF), hits, z, SUBSET + angle, nblk)
    write_half(sums, 0, shape, SUBSET + angle, measured, SUBSET + angle, proj, give_ref, nblk)


def keep_kernel(nblk, x_ref, hits, shape, measured, keep_ref, sums, proj):
    angle = SUBSET + halves()[0]
    for z in range(x_ref.shape[0]):
        add_half(sums, x_ref[z].astype(BF), hits, z, angle, nblk)
    write_half(sums, 0, shape, angle, measured, angle, proj, keep_ref, nblk)


def last_kernel(
    nblk, depth, x_ref, w_any, hits, shape, other_ref, part_ref, out_ref, near_ref, far_ref, w, proj, sems
):
    got = copies([w_any.at[z] for z in range(depth)], [w.at[z] for z in range(depth)], sems)
    angle = SUBSET + halves()[1]
    table = spread_half(other_ref, shape, angle, proj, nblk)
    for z in range(depth):
        update = (part_ref[z] + update_half(hits, z, angle, table, nblk)).T
        got[z].wait()
        tiles = x_ref[z] + w[z] * update
        out_ref[z] = tiles
        if z == 0 or z == depth - 1:
            edge = tiles.astype(BF)
            goes_far = odd_core() == (z != 0)

            @pl.when(goes_far)
            def _():
                far_ref[...] = edge

            @pl.when(jnp.logical_not(goes_far))
            def _():
                near_ref[...] = edge


def lanes_of(value):
    return lax.broadcasted_iota(jnp.int32, value.shape, 1)


def flows(here, after, there=None):
    width = here.shape[1]
    grad_z = after - here if there is None else (after - here) * there
    grad_x = jnp.where(lanes_of(here) == width - 1, 0.0, pltpu.roll(here, width - 1, 1) - here)
    scale = lax.rsqrt(grad_z * grad_z + grad_x * grad_x + 0.01)
    return grad_z * scale, grad_x * scale


def less_before(flow_x):
    return flow_x - jnp.where(lanes_of(flow_x) == 0, 0.0, pltpu.roll(flow_x, 1, 1))


RUN = 256


def inner_kernel(x_ref, near_ref, out_any, part_ref, done, sems):
    depth, rows, _ = x_ref.shape

    def finish(slices):
        sent = [pltpu.make_async_copy(done.at[z], out_any.at[z], sems.at[z]) for z in slices]
        for copy in sent:
            copy.start()
        for copy in sent:
            copy.wait()

    @pl.when(jnp.logical_not(odd_core()))
    def _():
        @pl.loop(0, rows // RUN)
        def _(i):
            spot = pl.ds(pl.multiple_of(i * RUN, RUN), RUN)
            here = x_ref[0, spot]
            before = None
            for z in range(depth):
                after = x_ref[z + 1, spot] if z + 1 < depth else near_ref[spot].astype(F32)
                flow_z, flow_x = flows(here, after)
                if z == 0:
                    part_ref[spot] = here + 0.2 * (flow_z + less_before(flow_x))
                else:
                    done[z, spot] = here + 0.2 * (flow_z - before + less_before(flow_x))
                here, before = after, flow_z

        finish(range(1, depth))

    @pl.when(odd_core())
    def _():
        @pl.loop(0, rows // RUN)
        def _(i):
            spot = pl.ds(pl.multiple_of(i * RUN, RUN), RUN)
            here = x_ref[0, spot]
            before, _ = flows(near_ref[spot].astype(F32), here)
            for z in range(depth - 1):
                after = x_ref[z + 1, spot]
                flow_z, flow_x = flows(here, after)
                done[z, spot] = here + 0.2 * (flow_z - before + less_before(flow_x))
                here, before = after, flow_z
            part_ref[spot] = here - 0.2 * before

        finish(range(depth - 1))


def outer_kernel(x_ref, part_ref, far_ref, _, out_any, done, sems):
    depth, rows, _ = x_ref.shape
    position = lax.axis_index("slab")

    def send(z, i):
        spot = pl.ds(i * RUN, RUN)
        return pltpu.make_async_copy(done.at[spot], out_any.at[z, spot], sems.at[i])

    @pl.when(jnp.logical_not(odd_core()))
    def _():
        there = jnp.where(position == 0, 0.0, 1.0)
        for i in range(rows // RUN):
            spot = pl.ds(i * RUN, RUN)
            flow_z, _ = flows(far_ref[spot].astype(F32), x_ref[0, spot], there)
            done[spot] = part_ref[spot] - 0.2 * flow_z
            send(0, i).start()
        for i in range(rows // RUN):
            send(0, i).wait()

    @pl.when(odd_core())
    def _():
        there = jnp.where(position == lax.axis_size("slab") - 1, 0.0, 1.0)
        for i in range(rows // RUN):
            spot = pl.ds(i * RUN, RUN)
            flow_z, flow_x = flows(x_ref[depth - 1, spot], far_ref[spot].astype(F32), there)
            done[spot] = part_ref[spot] + 0.2 * (flow_z + less_before(flow_x))
            send(depth - 1, i).start()
        for i in range(rows // RUN):
            send(depth - 1, i).wait()


def swap(value, bits):
    count = lax.axis_size("slab")
    return lax.ppermute(value, "slab", [(i, i ^ bits) for i in range(count)])


def reduce_and_share(keep, give, rays):
    quarters = (3, 5, 6)
    half = keep + swap(give, 1)
    arrived = [swap(half[1 + j].astype(BF), bits) for j, bits in enumerate(quarters)]
    total = half[0] + sum(a.astype(F32) for a in arrived)
    bit = 8
    while bit < lax.axis_size("slab"):
        total = total + swap(total.astype(BF), bit | 1).astype(F32)
        bit *= 2
    resid = (total * -rays).astype(BF)
    return jnp.stack([resid] + [swap(resid, bits) for bits in quarters])


def per_device(volume, voxel_weight, measured, ray_weight, footprint, hits):
    depth, rows, width = volume.shape
    count = lax.axis_size("slab")
    nblk = measured.shape[1] * count
    lists = hits.transpose(0, 2, 3, 1)
    piece = SUBSET * nblk // PIECES
    pieces = [jax.ShapeDtypeStruct((4, piece, width), F32)] * 2
    field = jax.ShapeDtypeStruct(volume.shape, F32)
    edge = jax.ShapeDtypeStruct((rows, width), BF)
    x_buf = pltpu.VMEM(volume.shape, F32)
    hits_buf = pltpu.VMEM(lists.shape, jnp.int32)
    shape_buf = pltpu.VMEM((SUBSET,) + footprint.shape[1:], BF)
    measured_buf = pltpu.VMEM((SUBSET,) + measured.shape[1:], F32)
    sums = pltpu.VMEM((SUBSET, nblk, width), F32)
    half_sums = pltpu.VMEM((2, nblk, width), F32)
    proj = pltpu.VMEM((2 * nblk, width), F32)
    rays = lax.dynamic_slice_in_dim(ray_weight, (own_piece() & 1) * piece, piece, 0)

    keep, give = pl.pallas_call(
        functools.partial(forward_kernel, nblk, depth),
        in_specs=[OUTSIDE] * 4,
        out_specs=[WHOLE] * 2,
        out_shape=pieces,
        scratch_shapes=[x_buf, hits_buf, shape_buf, measured_buf, sums, proj, pltpu.SemaphoreType.DMA((3 + depth,))],
        compiler_params=FIRST,
        name="forward",
    )(volume, lists, footprint, measured)
    def cost(flops):
        return pl.CostEstimate(flops=flops, bytes_accessed=2**20, transcendentals=0)

    def own_update(first, own):
        return pl.pallas_call(
            functools.partial(own_kernel, nblk, first),
            in_specs=[WHOLE] * 3,
            out_specs=WHOLE,
            out_shape=jax.ShapeDtypeStruct((depth, width, rows), F32),
            scratch_shapes=[proj],
            compiler_params=PARAMS,
            cost_estimate=cost(10**9),
            name="own",
        )(lists, footprint, own)

    own = reduce_and_share(keep, give, rays)
    other = swap(own, 1)
    part = own_update(0, own)
    x, give = pl.pallas_call(
        functools.partial(middle_kernel, nblk, depth),
        in_specs=[OUTSIDE] * 2 + [WHOLE] * 5,
        out_specs=[WHOLE] * 2,
        out_shape=[field, pieces[0]],
        scratch_shapes=[x_buf, x_buf, half_sums, proj, pltpu.SemaphoreType.DMA((2 * depth,))],
        compiler_params=MIDDLE,
        name="middle",
    )(volume, voxel_weight, lists, footprint, measured, other, part)
    keep = pl.pallas_call(
        functools.partial(keep_kernel, nblk),
        in_specs=[WHOLE] * 4,
        out_specs=WHOLE,
        out_shape=pieces[0],
        scratch_shapes=[half_sums, proj],
        compiler_params=PARAMS,
        cost_estimate=cost(10**9),
        name="keep",
    )(x, lists, footprint, measured)
    own = reduce_and_share(keep, give, rays)
    other = swap(own, 1)
    part = own_update(SUBSET, own)
    x, near, far = pl.pallas_call(
        functools.partial(last_kernel, nblk, depth),
        in_specs=[WHOLE] + [OUTSIDE] + [WHOLE] * 4,
        out_specs=[WHOLE] * 3,
        out_shape=[field, edge, edge],
        scratch_shapes=[x_buf, proj, pltpu.SemaphoreType.DMA((depth,))],
        compiler_params=PARAMS,
        name="last",
    )(x, voxel_weight, lists, footprint, other, part)
    far = lax.ppermute(far, "slab", [(i, min(max((i + 1) // 2 * 4 - 1 - i, 0), count - 1)) for i in range(count)])
    near = swap(near, 1)
    part = jax.ShapeDtypeStruct((rows, width), F32)
    out, part = pl.pallas_call(
        inner_kernel,
        in_specs=[WHOLE] * 2,
        out_specs=[OUTSIDE, WHOLE],
        out_shape=[field, part],
        scratch_shapes=[x_buf, pltpu.SemaphoreType.DMA((depth,))],
        compiler_params=PARAMS,
        cost_estimate=pl.CostEstimate(flops=3 * 10**9, bytes_accessed=8 * 2**20, transcendentals=0),
        name="inner",
    )(x, near)
    return pl.pallas_call(
        outer_kernel,
        in_specs=[WHOLE] * 3 + [OUTSIDE],
        out_specs=OUTSIDE,
        out_shape=field,
        input_output_aliases={3: 0},
        scratch_shapes=[pltpu.VMEM((rows, width), F32), pltpu.SemaphoreType.DMA((rows // RUN,))],
        compiler_params=PARAMS,
        name="outer",
    )(x, part, far, out)


def solution(mesh):
    return jax.shard_map(
        per_device,
        mesh=mesh,
        in_specs=(
            P(("parts", "slab"), None, None),
            P(("parts", "slab"), None, None),
            P("parts", "slab", None),
            P(),
            P(),
            P(("parts", "slab"), None, None, None),
        ),
        out_specs=P(("parts", "slab"), None, None),
        check_vma=False,
    )
```

```python
import functools

import jax
import jax.numpy as jnp
from jax import lax
from jax.experimental import pallas as pl
from jax.experimental.pallas import tpu as pltpu
from jax.sharding import PartitionSpec as P

SUBSET = 4
PIECES = 8
BF = jnp.bfloat16
F32 = jnp.float32
WHOLE = pl.BlockSpec(memory_space=pltpu.VMEM)
OUTSIDE = pl.BlockSpec(memory_space=pl.ANY)
FIRST = pltpu.CompilerParams(vmem_limit_bytes=int(53.2 * 2**20))
MIDDLE = pltpu.CompilerParams(vmem_limit_bytes=int(40 * 2**20))
PARAMS = pltpu.CompilerParams(vmem_limit_bytes=24 * 2**20)


def own_piece():
    position = lax.axis_index("slab")
    half = position
    for shift in (8, 4, 2, 1):
        half = half ^ (half >> shift)
    return (half & 1) * 4 + ((position >> 1) & 3)


def odd_core():
    return (lax.axis_index("slab") & 1) == 1


def split(value):
    high = value.astype(BF)
    return high, (value - high.astype(F32)).astype(BF)


def dot(a, b):
    return jnp.dot(a, b, preferred_element_type=F32)


def one_hots(hits, z, first, nblk):
    rows = lax.broadcasted_iota(jnp.int32, (nblk, hits.shape[3]), 0)
    return [jnp.where(rows == hits[z, first + a, 0:1, :], 1.0, 0.0).astype(BF) for a in range(SUBSET)]


def add_segments(sums, tiles, hits, z, first, nblk):
    for a, one_hot in enumerate(one_hots(hits, z, first, nblk)):
        part = dot(one_hot, tiles)
        sums[a] = part if z == 0 else sums[a] + part


def halves():
    half = own_piece() >> 2
    return half * 2, (1 - half) * 2


def add_half(sums, tiles, hits, z, first, nblk):
    rows = lax.broadcasted_iota(jnp.int32, (nblk, tiles.shape[0]), 0)
    for a in range(2):
        part = dot(jnp.where(rows == hits[z, first + a, 0:1, :], 1.0, 0.0).astype(BF), tiles)
        sums[a] = part if z == 0 else sums[a] + part


def write_half(sums, at, shape, shape_at, measured, measured_at, proj, out_ref, nblk):
    own = measured.shape[1]
    start = pl.multiple_of(lax.axis_index("slab") * own, own)
    totals = []
    for a in range(2):
        high, low = split(sums[at + a])
        both = jnp.concatenate([shape[shape_at + a, 0], shape[shape_at + a, 1]], axis=1)
        part = dot(high, both) + dot(low, both)
        near, far = part[:, :128], part[:, 128:]
        totals.append(near + jnp.concatenate([jnp.zeros_like(far[:1]), far[:-1]], axis=0))
    for a in range(2):
        proj[pl.ds(a * nblk, nblk)] = totals[a]
    for a in range(2):
        spot = pl.ds(a * nblk + start, own)
        proj[spot] = proj[spot] - measured[measured_at + a]
    rows = nblk // 2
    mine = own_piece() & 3
    for r in range(4):
        out_ref[r] = proj[pl.ds(pl.multiple_of((mine ^ r) * rows, rows), rows)]


def spread_half(pieces_ref, shape, at, resid, nblk):
    rows = nblk // 2
    mine = own_piece() & 3
    for r in range(4):
        resid[pl.ds(pl.multiple_of((mine ^ r) * rows, rows), rows)] = pieces_ref[r].astype(F32)
    contract = (((1,), (1,)), ((), ()))
    totals = []
    for a in range(2):
        part = resid[pl.ds(a * nblk, nblk)]
        after = jnp.concatenate([part[1:], jnp.zeros_like(part[:1])], axis=0)
        total = lax.dot_general(shape[at + a, 0], part.astype(BF), contract, preferred_element_type=F32)
        total += lax.dot_general(shape[at + a, 1], after.astype(BF), contract, preferred_element_type=F32)
        totals.append(total.astype(BF))
    return jnp.concatenate(totals, axis=1)


def update_half(hits, z, first, table, nblk):
    rows = lax.broadcasted_iota(jnp.int32, (nblk, hits.shape[3]), 0)
    hot = [jnp.where(rows == hits[z, first + a, 0:1, :], 1.0, 0.0).astype(BF) for a in range(2)]
    return dot(table, jnp.concatenate(hot, axis=0))


def copies(sources, targets, sems):
    started = [pltpu.make_async_copy(s, t, sems.at[i]) for i, (s, t) in enumerate(zip(sources, targets))]
    for copy in started:
        copy.start()
    return started


def forward_kernel(
    nblk, depth, x_any, hits_any, shape_any, measured_any, keep_ref, give_ref, x, hits, shape, measured, sums, proj, sems
):
    got = copies(
        [hits_any, x_any.at[0], shape_any.at[pl.ds(0, SUBSET)], measured_any.at[pl.ds(0, SUBSET)]]
        + [x_any.at[z] for z in range(1, depth)],
        [hits, x.at[0], shape, measured] + [x.at[z] for z in range(1, depth)],
        sems,
    )
    got[0].wait()
    for z in range(depth):
        got[1 if z == 0 else 3 + z].wait()
        add_segments(sums, x[z].astype(BF), hits, z, 0, nblk)
    got[2].wait()
    got[3].wait()
    own, other = halves()
    write_half(sums, other, shape, other, measured, other, proj, give_ref, nblk)
    write_half(sums, own, shape, own, measured, own, proj, keep_ref, nblk)


def own_kernel(nblk, first, hits, shape, own_ref, out_ref, resid):
    angle = first + halves()[0]
    table = spread_half(own_ref, shape, angle, resid, nblk)
    for z in range(hits.shape[0]):
        out_ref[z] = update_half(hits, z, angle, table, nblk)


def middle_kernel(
    nblk, depth, x_any, w_any, hits, shape, measured, other_ref, part_ref, out_ref, give_ref,
    x, w, sums, proj, sems,
):
    got = copies(
        [x_any.at[z] for z in range(depth)] + [w_any.at[z] for z in range(depth)],
        [x.at[z] for z in range(depth)] + [w.at[z] for z in range(depth)],
        sems,
    )
    angle = halves()[1]
    table = spread_half(other_ref, shape, angle, proj, nblk)
    for z in range(depth):
        update = (part_ref[z] + update_half(hits, z, angle, table, nblk)).T
        got[z].wait()
        got[depth + z].wait()
        tiles = x[z] + w[z] * update
        out_ref[z] = tiles
        add_half(sums, tiles.astype(BF), hits, z, SUBSET + angle, nblk)
    write_half(sums, 0, shape, SUBSET + angle, measured, SUBSET + angle, proj, give_ref, nblk)


def keep_kernel(nblk, x_ref, hits, shape, measured, keep_ref, sums, proj):
    angle = SUBSET + halves()[0]
    for z in range(x_ref.shape[0]):
        add_half(sums, x_ref[z].astype(BF), hits, z, angle, nblk)
    write_half(sums, 0, shape, angle, measured, angle, proj, keep_ref, nblk)


def far_kernel(nblk, depth, x_ref, w_any, hits, shape, other_ref, part_ref, far_ref, table, w, proj, sems):
    far = jnp.where(odd_core(), depth - 1, 0)
    got = copies([w_any.at[far]], [w], sems)
    angle = SUBSET + halves()[1]
    table[...] = spread_half(other_ref, shape, angle, proj, nblk)
    update = (part_ref[far] + update_half(hits, far, angle, table[...], nblk)).T
    got[0].wait()
    far_ref[...] = (x_ref[far] + w[...] * update).astype(BF)


def last_kernel(nblk, depth, x_ref, w_any, hits, table, part_ref, out_ref, near_ref, w, sems):
    got = copies([w_any.at[z] for z in range(depth)], [w.at[z] for z in range(depth)], sems)
    angle = SUBSET + halves()[1]
    for z in range(depth):
        update = (part_ref[z] + update_half(hits, z, angle, table[...], nblk)).T
        got[z].wait()
        tiles = x_ref[z] + w[z] * update
        out_ref[z] = tiles
        if z == 0 or z == depth - 1:

            @pl.when(odd_core() == (z == 0))
            def _():
                near_ref[...] = tiles.astype(BF)


def lanes_of(value):
    return lax.broadcasted_iota(jnp.int32, value.shape, 1)


def grad_along(here):
    width = here.shape[1]
    return jnp.where(lanes_of(here) == width - 1, 0.0, pltpu.roll(here, width - 1, 1) - here)


def flows(here, after, there=None, grad_x=None):
    grad_z = after - here if there is None else (after - here) * there
    grad_x = grad_along(here) if grad_x is None else grad_x
    scale = lax.rsqrt(grad_z * grad_z + grad_x * grad_x + 0.01)
    return grad_z * scale, grad_x * scale


def less_before(flow_x):
    return flow_x - jnp.where(lanes_of(flow_x) == 0, 0.0, pltpu.roll(flow_x, 1, 1))


RUN = 256


def inner_kernel(x_ref, *refs):
    depth, rows, _ = x_ref.shape
    near_refs, (out_any, part_ref, grad_ref, done, sems) = refs[:-5], refs[-5:]
    each = rows // len(near_refs)

    def near_run(i):
        inside = pl.ds(pl.multiple_of(lax.rem(i * RUN, each), RUN), RUN)
        value = near_refs[0][inside]
        for n, ref in enumerate(near_refs[1:]):
            value = jnp.where(i * RUN >= (n + 1) * each, ref[inside], value)
        return value.astype(F32)

    def finish(slices):
        sent = [pltpu.make_async_copy(done.at[z], out_any.at[z], sems.at[z]) for z in slices]
        for copy in sent:
            copy.start()
        for copy in sent:
            copy.wait()

    @pl.when(jnp.logical_not(odd_core()))
    def _():
        @pl.loop(0, rows // RUN)
        def _(i):
            spot = pl.ds(pl.multiple_of(i * RUN, RUN), RUN)
            here = x_ref[0, spot]
            before = None
            for z in range(depth):
                after = x_ref[z + 1, spot] if z + 1 < depth else near_run(i)
                flow_z, flow_x = flows(here, after)
                if z == 0:
                    part_ref[spot] = here + 0.2 * (flow_z + less_before(flow_x))
                else:
                    done[z, spot] = here + 0.2 * (flow_z - before + less_before(flow_x))
                here, before = after, flow_z

        finish(range(1, depth))

    @pl.when(odd_core())
    def _():
        @pl.loop(0, rows // RUN)
        def _(i):
            spot = pl.ds(pl.multiple_of(i * RUN, RUN), RUN)
            here = x_ref[0, spot]
            before, _ = flows(near_run(i), here)
            for z in range(depth - 1):
                after = x_ref[z + 1, spot]
                flow_z, flow_x = flows(here, after)
                done[z, spot] = here + 0.2 * (flow_z - before + less_before(flow_x))
                here, before = after, flow_z
            part_ref[spot] = here - 0.2 * before
            grad_ref[spot] = grad_along(here)

        finish(range(depth - 1))


def outer_kernel(x_ref, part_ref, grad_ref, far_ref, _, out_any, done, sems):
    depth, rows, _ = x_ref.shape
    position = lax.axis_index("slab")

    def send(z, i):
        spot = pl.ds(i * RUN, RUN)
        return pltpu.make_async_copy(done.at[spot], out_any.at[z, spot], sems.at[i])

    @pl.when(jnp.logical_not(odd_core()))
    def _():
        there = jnp.where(position == 0, 0.0, 1.0)
        for i in range(rows // RUN):
            spot = pl.ds(i * RUN, RUN)
            flow_z, _ = flows(far_ref[spot].astype(F32), x_ref[0, spot], there)
            done[spot] = part_ref[spot] - 0.2 * flow_z
            send(0, i).start()
        for i in range(rows // RUN):
            send(0, i).wait()

    @pl.when(odd_core())
    def _():
        there = jnp.where(position == lax.axis_size("slab") - 1, 0.0, 1.0)
        for i in range(rows // RUN):
            spot = pl.ds(i * RUN, RUN)
            flow_z, flow_x = flows(x_ref[depth - 1, spot], far_ref[spot].astype(F32), there, grad_ref[spot])
            done[spot] = part_ref[spot] + 0.2 * (flow_z + less_before(flow_x))
            send(depth - 1, i).start()
        for i in range(rows // RUN):
            send(depth - 1, i).wait()


def swap(value, bits):
    count = lax.axis_size("slab")
    return lax.ppermute(value, "slab", [(i, i ^ bits) for i in range(count)])


def reduce_and_share(keep, give, rays):
    quarters = (3, 5, 6)
    half = keep + swap(give, 1)
    arrived = [swap(half[1 + j].astype(BF), bits) for j, bits in enumerate(quarters)]
    total = half[0] + sum(a.astype(F32) for a in arrived)
    bit = 8
    while bit < lax.axis_size("slab"):
        total = total + swap(total.astype(BF), bit | 1).astype(F32)
        bit *= 2
    resid = (total * -rays).astype(BF)
    return jnp.stack([resid] + [swap(resid, bits) for bits in quarters])


def per_device(volume, voxel_weight, measured, ray_weight, footprint, hits):
    depth, rows, width = volume.shape
    count = lax.axis_size("slab")
    nblk = measured.shape[1] * count
    lists = hits.transpose(0, 2, 3, 1)
    piece = SUBSET * nblk // PIECES
    pieces = [jax.ShapeDtypeStruct((4, piece, width), F32)] * 2
    field = jax.ShapeDtypeStruct(volume.shape, F32)
    edge = jax.ShapeDtypeStruct((rows, width), BF)
    x_buf = pltpu.VMEM(volume.shape, F32)
    hits_buf = pltpu.VMEM(lists.shape, jnp.int32)
    shape_buf = pltpu.VMEM((SUBSET,) + footprint.shape[1:], BF)
    measured_buf = pltpu.VMEM((SUBSET,) + measured.shape[1:], F32)
    sums = pltpu.VMEM((SUBSET, nblk, width), F32)
    half_sums = pltpu.VMEM((2, nblk, width), F32)
    proj = pltpu.VMEM((2 * nblk, width), F32)
    rays = lax.dynamic_slice_in_dim(ray_weight, (own_piece() & 1) * piece, piece, 0)

    keep, give = pl.pallas_call(
        functools.partial(forward_kernel, nblk, depth),
        in_specs=[OUTSIDE] * 4,
        out_specs=[WHOLE] * 2,
        out_shape=pieces,
        scratch_shapes=[x_buf, hits_buf, shape_buf, measured_buf, sums, proj, pltpu.SemaphoreType.DMA((3 + depth,))],
        compiler_params=FIRST,
        name="forward",
    )(volume, lists, footprint, measured)
    def cost(flops):
        return pl.CostEstimate(flops=flops, bytes_accessed=2**10 if flops < 10**6 else 2**20, transcendentals=0)

    def own_update(first, own):
        return pl.pallas_call(
            functools.partial(own_kernel, nblk, first),
            in_specs=[WHOLE] * 3,
            out_specs=WHOLE,
            out_shape=jax.ShapeDtypeStruct((depth, width, rows), F32),
            scratch_shapes=[proj],
            compiler_params=PARAMS,
            cost_estimate=cost(10**9),
            name="own",
        )(lists, footprint, own)

    own = reduce_and_share(keep, give, rays)
    other = swap(own, 1)
    part = own_update(0, own)
    x, give = pl.pallas_call(
        functools.partial(middle_kernel, nblk, depth),
        in_specs=[OUTSIDE] * 2 + [WHOLE] * 5,
        out_specs=[WHOLE] * 2,
        out_shape=[field, pieces[0]],
        scratch_shapes=[x_buf, x_buf, half_sums, proj, pltpu.SemaphoreType.DMA((2 * depth,))],
        compiler_params=MIDDLE,
        name="middle",
    )(volume, voxel_weight, lists, footprint, measured, other, part)
    keep = pl.pallas_call(
        functools.partial(keep_kernel, nblk),
        in_specs=[WHOLE] * 4,
        out_specs=WHOLE,
        out_shape=pieces[0],
        scratch_shapes=[half_sums, proj],
        compiler_params=PARAMS,
        cost_estimate=cost(10**9),
        name="keep",
    )(x, lists, footprint, measured)
    own = reduce_and_share(keep, give, rays)
    other = swap(own, 1)
    part = own_update(SUBSET, own)
    far, table = pl.pallas_call(
        functools.partial(far_kernel, nblk, depth),
        in_specs=[WHOLE] + [OUTSIDE] + [WHOLE] * 4,
        out_specs=[WHOLE] * 2,
        out_shape=[edge, jax.ShapeDtypeStruct((width, 2 * nblk), BF)],
        scratch_shapes=[pltpu.VMEM((rows, width), F32), proj, pltpu.SemaphoreType.DMA((1,))],
        compiler_params=PARAMS,
        name="far",
    )(x, voxel_weight, lists, footprint, other, part)
    far = lax.ppermute(far, "slab", [(i, min(max((i + 1) // 2 * 4 - 1 - i, 0), count - 1)) for i in range(count)])
    x, near = pl.pallas_call(
        functools.partial(last_kernel, nblk, depth),
        in_specs=[WHOLE] + [OUTSIDE] + [WHOLE] * 3,
        out_specs=[WHOLE] * 2,
        out_shape=[field, edge],
        scratch_shapes=[x_buf, pltpu.SemaphoreType.DMA((depth,))],
        compiler_params=PARAMS,
        cost_estimate=cost(10**3),
        name="last",
    )(x, voxel_weight, lists, table, part)
    quarter = rows // 4
    near = [swap(near[i * quarter : (i + 1) * quarter], 1) for i in range(4)]
    part = jax.ShapeDtypeStruct((rows, width), F32)
    out, part, grad = pl.pallas_call(
        inner_kernel,
        in_specs=[WHOLE] * (1 + len(near)),
        out_specs=[OUTSIDE, WHOLE, WHOLE],
        out_shape=[field, part, part],
        scratch_shapes=[x_buf, pltpu.SemaphoreType.DMA((depth,))],
        compiler_params=PARAMS,
        cost_estimate=cost(10**3),
        name="inner",
    )(x, *near)
    return pl.pallas_call(
        outer_kernel,
        in_specs=[WHOLE] * 4 + [OUTSIDE],
        out_specs=OUTSIDE,
        out_shape=field,
        input_output_aliases={4: 0},
        scratch_shapes=[pltpu.VMEM((rows, width), F32), pltpu.SemaphoreType.DMA((rows // RUN,))],
        compiler_params=PARAMS,
        name="outer",
    )(x, part, grad, far, out)


def solution(mesh):
    return jax.shard_map(
        per_device,
        mesh=mesh,
        in_specs=(
            P(("parts", "slab"), None, None),
            P(("parts", "slab"), None, None),
            P("parts", "slab", None),
            P(),
            P(),
            P(("parts", "slab"), None, None, None),
        ),
        out_specs=P(("parts", "slab"), None, None),
        check_vma=False,
    )
```

```python
import functools

import jax
import jax.numpy as jnp
from jax import lax
from jax.experimental import pallas as pl
from jax.experimental.pallas import tpu as pltpu
from jax.sharding import PartitionSpec as P

SUBSET = 4
PIECES = 8
BF = jnp.bfloat16
F32 = jnp.float32
WHOLE = pl.BlockSpec(memory_space=pltpu.VMEM)
OUTSIDE = pl.BlockSpec(memory_space=pl.ANY)
FIRST = pltpu.CompilerParams(vmem_limit_bytes=int(53.2 * 2**20))
MIDDLE = pltpu.CompilerParams(vmem_limit_bytes=int(40 * 2**20))
PARAMS = pltpu.CompilerParams(vmem_limit_bytes=24 * 2**20)


def own_piece():
    position = lax.axis_index("slab")
    half = position
    for shift in (8, 4, 2, 1):
        half = half ^ (half >> shift)
    return (half & 1) * 4 + ((position >> 1) & 3)


def odd_core():
    return (lax.axis_index("slab") & 1) == 1


def split(value):
    high = value.astype(BF)
    return high, (value - high.astype(F32)).astype(BF)


def dot(a, b):
    return jnp.dot(a, b, preferred_element_type=F32)


def one_hots(hits, z, first, nblk):
    rows = lax.broadcasted_iota(jnp.int32, (nblk, hits.shape[3]), 0)
    return [jnp.where(rows == hits[z, first + a, 0:1, :], 1.0, 0.0).astype(BF) for a in range(SUBSET)]


def add_segments(sums, tiles, hits, z, first, nblk):
    for a, one_hot in enumerate(one_hots(hits, z, first, nblk)):
        part = dot(one_hot, tiles)
        sums[a] = part if z == 0 else sums[a] + part


def halves():
    half = own_piece() >> 2
    return half * 2, (1 - half) * 2


def add_half(sums, tiles, hits, z, first, nblk):
    rows = lax.broadcasted_iota(jnp.int32, (nblk, tiles.shape[0]), 0)
    for a in range(2):
        part = dot(jnp.where(rows == hits[z, first + a, 0:1, :], 1.0, 0.0).astype(BF), tiles)
        sums[a] = part if z == 0 else sums[a] + part


def write_half(sums, at, shape, shape_at, measured, measured_at, proj, out_ref, nblk):
    own = measured.shape[1]
    start = pl.multiple_of(lax.axis_index("slab") * own, own)
    totals = []
    for a in range(2):
        high, low = split(sums[at + a])
        both = jnp.concatenate([shape[shape_at + a, 0], shape[shape_at + a, 1]], axis=1)
        part = dot(high, both) + dot(low, both)
        near, far = part[:, :128], part[:, 128:]
        totals.append(near + jnp.concatenate([jnp.zeros_like(far[:1]), far[:-1]], axis=0))
    for a in range(2):
        proj[pl.ds(a * nblk, nblk)] = totals[a]
    for a in range(2):
        spot = pl.ds(a * nblk + start, own)
        proj[spot] = proj[spot] - measured[measured_at + a]
    rows = nblk // 2
    mine = own_piece() & 3
    for r in range(4):
        out_ref[r] = proj[pl.ds(pl.multiple_of((mine ^ r) * rows, rows), rows)]


def spread_half(pieces_ref, shape, at, resid, nblk):
    rows = nblk // 2
    mine = own_piece() & 3
    for r in range(4):
        resid[pl.ds(pl.multiple_of((mine ^ r) * rows, rows), rows)] = pieces_ref[r].astype(F32)
    contract = (((1,), (1,)), ((), ()))
    totals = []
    for a in range(2):
        part = resid[pl.ds(a * nblk, nblk)]
        after = jnp.concatenate([part[1:], jnp.zeros_like(part[:1])], axis=0)
        total = lax.dot_general(shape[at + a, 0], part.astype(BF), contract, preferred_element_type=F32)
        total += lax.dot_general(shape[at + a, 1], after.astype(BF), contract, preferred_element_type=F32)
        totals.append(total.astype(BF))
    return jnp.concatenate(totals, axis=1)


def update_half(hits, z, first, table, nblk):
    rows = lax.broadcasted_iota(jnp.int32, (nblk, hits.shape[3]), 0)
    hot = [jnp.where(rows == hits[z, first + a, 0:1, :], 1.0, 0.0).astype(BF) for a in range(2)]
    return dot(table, jnp.concatenate(hot, axis=0))


def copies(sources, targets, sems):
    started = [pltpu.make_async_copy(s, t, sems.at[i]) for i, (s, t) in enumerate(zip(sources, targets))]
    for copy in started:
        copy.start()
    return started


def forward_kernel(
    nblk, depth, x_any, hits_any, shape_any, measured_any, keep_ref, give_ref, x, hits, shape, measured, sums, proj, sems
):
    got = copies(
        [hits_any, x_any.at[0], shape_any.at[pl.ds(0, SUBSET)], measured_any.at[pl.ds(0, SUBSET)]]
        + [x_any.at[z] for z in range(1, depth)],
        [hits, x.at[0], shape, measured] + [x.at[z] for z in range(1, depth)],
        sems,
    )
    got[0].wait()
    for z in range(depth):
        got[1 if z == 0 else 3 + z].wait()
        add_segments(sums, x[z].astype(BF), hits, z, 0, nblk)
    got[2].wait()
    got[3].wait()
    own, other = halves()
    write_half(sums, other, shape, other, measured, other, proj, give_ref, nblk)
    write_half(sums, own, shape, own, measured, own, proj, keep_ref, nblk)


def own_kernel(nblk, first, hits, shape, own_ref, out_ref, resid):
    angle = first + halves()[0]
    table = spread_half(own_ref, shape, angle, resid, nblk)
    for z in range(hits.shape[0]):
        out_ref[z] = update_half(hits, z, angle, table, nblk)


def middle_kernel(
    nblk, depth, x_any, w_any, hits, shape, measured, other_ref, part_ref, out_ref, give_ref,
    x, w, sums, proj, sems,
):
    got = copies(
        [array.at[z] for z in range(depth) for array in (x_any, w_any)],
        [array.at[z] for z in range(depth) for array in (x, w)],
        sems,
    )
    angle = halves()[1]
    table = spread_half(other_ref, shape, angle, proj, nblk)
    for z in range(depth):
        update = (part_ref[z] + update_half(hits, z, angle, table, nblk)).T
        got[2 * z].wait()
        got[2 * z + 1].wait()
        tiles = x[z] + w[z] * update
        out_ref[z] = tiles
        add_half(sums, tiles.astype(BF), hits, z, SUBSET + angle, nblk)
    write_half(sums, 0, shape, SUBSET + angle, measured, SUBSET + angle, proj, give_ref, nblk)


def keep_kernel(nblk, x_ref, hits, shape, measured, keep_ref, sums, proj):
    angle = SUBSET + halves()[0]
    for z in range(x_ref.shape[0]):
        add_half(sums, x_ref[z].astype(BF), hits, z, angle, nblk)
    write_half(sums, 0, shape, angle, measured, angle, proj, keep_ref, nblk)


def far_kernel(nblk, depth, x_ref, w_any, hits, shape, other_ref, part_ref, far_ref, table, w, proj, sems):
    far = jnp.where(odd_core(), depth - 1, 0)
    got = copies([w_any.at[far]], [w], sems)
    angle = SUBSET + halves()[1]
    table[...] = spread_half(other_ref, shape, angle, proj, nblk)
    update = (part_ref[far] + update_half(hits, far, angle, table[...], nblk)).T
    got[0].wait()
    far_ref[...] = (x_ref[far] + w[...] * update).astype(BF)


def last_kernel(nblk, depth, x_ref, w_any, hits, table, part_ref, out_ref, near_ref, w, sems):
    got = copies([w_any.at[z] for z in range(depth)], [w.at[z] for z in range(depth)], sems)
    angle = SUBSET + halves()[1]
    for z in range(depth):
        update = (part_ref[z] + update_half(hits, z, angle, table[...], nblk)).T
        got[z].wait()
        tiles = x_ref[z] + w[z] * update
        out_ref[z] = tiles
        if z == 0 or z == depth - 1:

            @pl.when(odd_core() == (z == 0))
            def _():
                near_ref[...] = tiles.astype(BF)


def lanes_of(value):
    return lax.broadcasted_iota(jnp.int32, value.shape, 1)


def grad_along(here):
    width = here.shape[1]
    return jnp.where(lanes_of(here) == width - 1, 0.0, pltpu.roll(here, width - 1, 1) - here)


def flows(here, after, there=None, grad_x=None):
    grad_z = after - here if there is None else (after - here) * there
    grad_x = grad_along(here) if grad_x is None else grad_x
    scale = lax.rsqrt(grad_z * grad_z + grad_x * grad_x + 0.01)
    return grad_z * scale, grad_x * scale


def less_before(flow_x):
    return flow_x - jnp.where(lanes_of(flow_x) == 0, 0.0, pltpu.roll(flow_x, 1, 1))


RUN = 256


def inner_kernel(x_ref, *refs):
    depth, rows, _ = x_ref.shape
    near_refs, (out_any, part_ref, grad_ref, done, sems) = refs[:-5], refs[-5:]
    each = rows // len(near_refs)

    def near_run(i):
        inside = pl.ds(pl.multiple_of(lax.rem(i * RUN, each), RUN), RUN)
        value = near_refs[0][inside]
        for n, ref in enumerate(near_refs[1:]):
            value = jnp.where(i * RUN >= (n + 1) * each, ref[inside], value)
        return value.astype(F32)

    def finish(slices):
        sent = [pltpu.make_async_copy(done.at[z], out_any.at[z], sems.at[z]) for z in slices]
        for copy in sent:
            copy.start()
        for copy in sent:
            copy.wait()

    @pl.when(jnp.logical_not(odd_core()))
    def _():
        @pl.loop(0, rows // RUN)
        def _(i):
            spot = pl.ds(pl.multiple_of(i * RUN, RUN), RUN)
            here = x_ref[0, spot]
            before = None
            for z in range(depth):
                after = x_ref[z + 1, spot] if z + 1 < depth else near_run(i)
                flow_z, flow_x = flows(here, after)
                if z == 0:
                    part_ref[spot] = here + 0.2 * (flow_z + less_before(flow_x))
                else:
                    done[z, spot] = here + 0.2 * (flow_z - before + less_before(flow_x))
                here, before = after, flow_z

        finish(range(1, depth))

    @pl.when(odd_core())
    def _():
        @pl.loop(0, rows // RUN)
        def _(i):
            spot = pl.ds(pl.multiple_of(i * RUN, RUN), RUN)
            here = x_ref[0, spot]
            before, _ = flows(near_run(i), here)
            for z in range(depth - 1):
                after = x_ref[z + 1, spot]
                flow_z, flow_x = flows(here, after)
                done[z, spot] = here + 0.2 * (flow_z - before + less_before(flow_x))
                here, before = after, flow_z
            part_ref[spot] = here - 0.2 * before
            grad_ref[spot] = grad_along(here)

        finish(range(depth - 1))


def outer_kernel(x_ref, part_ref, grad_ref, far_ref, _, out_any, done, sems):
    depth, rows, _ = x_ref.shape
    position = lax.axis_index("slab")

    def send(z, i):
        spot = pl.ds(i * RUN, RUN)
        return pltpu.make_async_copy(done.at[spot], out_any.at[z, spot], sems.at[i])

    @pl.when(jnp.logical_not(odd_core()))
    def _():
        there = jnp.where(position == 0, 0.0, 1.0)
        for i in range(rows // RUN):
            spot = pl.ds(i * RUN, RUN)
            flow_z, _ = flows(far_ref[spot].astype(F32), x_ref[0, spot], there)
            done[spot] = part_ref[spot] - 0.2 * flow_z
            send(0, i).start()
        for i in range(rows // RUN):
            send(0, i).wait()

    @pl.when(odd_core())
    def _():
        there = jnp.where(position == lax.axis_size("slab") - 1, 0.0, 1.0)
        for i in range(rows // RUN):
            spot = pl.ds(i * RUN, RUN)
            flow_z, flow_x = flows(x_ref[depth - 1, spot], far_ref[spot].astype(F32), there, grad_ref[spot])
            done[spot] = part_ref[spot] + 0.2 * (flow_z + less_before(flow_x))
            send(depth - 1, i).start()
        for i in range(rows // RUN):
            send(depth - 1, i).wait()


def swap(value, bits):
    count = lax.axis_size("slab")
    return lax.ppermute(value, "slab", [(i, i ^ bits) for i in range(count)])


def reduce_and_share(keep, give, rays):
    quarters = (3, 5, 6)
    half = keep + swap(give, 1)
    arrived = [swap(half[1 + j].astype(BF), bits) for j, bits in enumerate(quarters)]
    total = half[0] + sum(a.astype(F32) for a in arrived)
    bit = 8
    while bit < lax.axis_size("slab"):
        total = total + swap(total.astype(BF), bit | 1).astype(F32)
        bit *= 2
    resid = (total * -rays).astype(BF)
    return jnp.stack([resid] + [swap(resid, bits) for bits in quarters])


def per_device(volume, voxel_weight, measured, ray_weight, footprint, hits):
    depth, rows, width = volume.shape
    count = lax.axis_size("slab")
    nblk = measured.shape[1] * count
    lists = hits.transpose(0, 2, 3, 1)
    piece = SUBSET * nblk // PIECES
    pieces = [jax.ShapeDtypeStruct((4, piece, width), F32)] * 2
    field = jax.ShapeDtypeStruct(volume.shape, F32)
    edge = jax.ShapeDtypeStruct((rows, width), BF)
    x_buf = pltpu.VMEM(volume.shape, F32)
    hits_buf = pltpu.VMEM(lists.shape, jnp.int32)
    shape_buf = pltpu.VMEM((SUBSET,) + footprint.shape[1:], BF)
    measured_buf = pltpu.VMEM((SUBSET,) + measured.shape[1:], F32)
    sums = pltpu.VMEM((SUBSET, nblk, width), F32)
    half_sums = pltpu.VMEM((2, nblk, width), F32)
    proj = pltpu.VMEM((2 * nblk, width), F32)
    rays = lax.dynamic_slice_in_dim(ray_weight, (own_piece() & 1) * piece, piece, 0)

    keep, give = pl.pallas_call(
        functools.partial(forward_kernel, nblk, depth),
        in_specs=[OUTSIDE] * 4,
        out_specs=[WHOLE] * 2,
        out_shape=pieces,
        scratch_shapes=[x_buf, hits_buf, shape_buf, measured_buf, sums, proj, pltpu.SemaphoreType.DMA((3 + depth,))],
        compiler_params=FIRST,
        name="forward",
    )(volume, lists, footprint, measured)
    def cost(flops):
        return pl.CostEstimate(flops=flops, bytes_accessed=2**10 if flops < 10**6 else 2**20, transcendentals=0)

    def own_update(first, own):
        return pl.pallas_call(
            functools.partial(own_kernel, nblk, first),
            in_specs=[WHOLE] * 3,
            out_specs=WHOLE,
            out_shape=jax.ShapeDtypeStruct((depth, width, rows), F32),
            scratch_shapes=[proj],
            compiler_params=PARAMS,
            cost_estimate=cost(10**9),
            name="own",
        )(lists, footprint, own)

    own = reduce_and_share(keep, give, rays)
    other = swap(own, 1)
    part = own_update(0, own)
    x, give = pl.pallas_call(
        functools.partial(middle_kernel, nblk, depth),
        in_specs=[OUTSIDE] * 2 + [WHOLE] * 5,
        out_specs=[WHOLE] * 2,
        out_shape=[field, pieces[0]],
        scratch_shapes=[x_buf, x_buf, half_sums, proj, pltpu.SemaphoreType.DMA((2 * depth,))],
        compiler_params=MIDDLE,
        name="middle",
    )(volume, voxel_weight, lists, footprint, measured, other, part)
    keep = pl.pallas_call(
        functools.partial(keep_kernel, nblk),
        in_specs=[WHOLE] * 4,
        out_specs=WHOLE,
        out_shape=pieces[0],
        scratch_shapes=[half_sums, proj],
        compiler_params=PARAMS,
        cost_estimate=cost(10**9),
        name="keep",
    )(x, lists, footprint, measured)
    own = reduce_and_share(keep, give, rays)
    other = swap(own, 1)
    part = own_update(SUBSET, own)
    far, table = pl.pallas_call(
        functools.partial(far_kernel, nblk, depth),
        in_specs=[WHOLE] + [OUTSIDE] + [WHOLE] * 4,
        out_specs=[WHOLE] * 2,
        out_shape=[edge, jax.ShapeDtypeStruct((width, 2 * nblk), BF)],
        scratch_shapes=[pltpu.VMEM((rows, width), F32), proj, pltpu.SemaphoreType.DMA((1,))],
        compiler_params=PARAMS,
        name="far",
    )(x, voxel_weight, lists, footprint, other, part)
    far = lax.ppermute(far, "slab", [(i, ((i + 1) // 2 * 4 - 1 - i) % count) for i in range(count)])
    x, near = pl.pallas_call(
        functools.partial(last_kernel, nblk, depth),
        in_specs=[WHOLE] + [OUTSIDE] + [WHOLE] * 3,
        out_specs=[WHOLE] * 2,
        out_shape=[field, edge],
        scratch_shapes=[x_buf, pltpu.SemaphoreType.DMA((depth,))],
        compiler_params=PARAMS,
        cost_estimate=cost(10**3),
        name="last",
    )(x, voxel_weight, lists, table, part)
    quarter = rows // 4
    near = [swap(near[i * quarter : (i + 1) * quarter], 1) for i in range(4)]
    part = jax.ShapeDtypeStruct((rows, width), F32)
    out, part, grad = pl.pallas_call(
        inner_kernel,
        in_specs=[WHOLE] * (1 + len(near)),
        out_specs=[OUTSIDE, WHOLE, WHOLE],
        out_shape=[field, part, part],
        scratch_shapes=[x_buf, pltpu.SemaphoreType.DMA((depth,))],
        compiler_params=PARAMS,
        cost_estimate=cost(10**3),
        name="inner",
    )(x, *near)
    return pl.pallas_call(
        outer_kernel,
        in_specs=[WHOLE] * 4 + [OUTSIDE],
        out_specs=OUTSIDE,
        out_shape=field,
        input_output_aliases={4: 0},
        scratch_shapes=[pltpu.VMEM((rows, width), F32), pltpu.SemaphoreType.DMA((rows // RUN,))],
        compiler_params=PARAMS,
        name="outer",
    )(x, part, grad, far, out)


def solution(mesh):
    return jax.shard_map(
        per_device,
        mesh=mesh,
        in_specs=(
            P(("parts", "slab"), None, None),
            P(("parts", "slab"), None, None),
            P("parts", "slab", None),
            P(),
            P(),
            P(("parts", "slab"), None, None, None),
        ),
        out_specs=P(("parts", "slab"), None, None),
        check_vma=False,
    )
```
